32 devices in a mesh: groups: 2 (over y), edge: 4 (over z), trip: 2 (over x), sub: 2 (over core).
Axes of the slice: x: 2, y: 2, z: 4, core: 2. Of those that a mesh axis runs over, the one named last changes fastest.
Arguments:
- edge_feat: float32 [128, 128, 512], P(('groups', 'edge'), ('trip', 'sub')), parts along dimension 0, may hold values from -6 to 6
- edge_counts: int32 [128], P(('groups', 'edge')), parts along dimension 0, may hold values from 64 to 128
- reverse: int32 [128], P('groups'), parts along dimension 0, may hold values from 0 to 63, as said below
- patterns: int32 [8, 4, 64, 2], P(('groups', 'edge'), ('trip', 'sub')), parts along dimension 0, may hold values from 0 to 15
- trip_count: int32 [8, 4], P(('groups', 'edge'), ('trip', 'sub')), parts along dimension 0, may hold values from 16 to 64, as said below
- coef: float32 [8, 4, 64, 128, 128], P(('groups', 'edge'), ('trip', 'sub')), parts along dimension 0, may hold values from -0.1875 to 0.1875
- down_weight: float32 [3, 512, 256], replicated, may hold values from -0.25 to 0.25
- up_weight: float32 [3, 256, 512], replicated, may hold values from -0.375 to 0.375
- dense_weight: float32 [3, 512, 512], replicated, may hold values from -0.25 to 0.25
Outputs:
- edge_out: float32 [128, 128, 512], P(('groups', 'edge'), ('trip', 'sub')), parts along dimension 0
The draws below stay inside these ranges and needn't reach their ends.
There are 2 independent parts, one for each index of `groups`. The reference program is written for one: setup_inputs(seed, part) draws one part's arguments, and reference() takes and returns one part's arrays. A program takes and returns all parts, laid end to end along the dimension named above; an argument that names none is the same for every part. Nothing has to cross between parts.
Inputs may be any that keep to these rules, and one draw needn't show every extreme that they name: reverse is an involution without fixed points; reverse[c] lies on another index of edge than c; from one index of edge at most 8 clusters have their reverse on one other index, and that many in every draw. `trip_count`: some device has all 64 slots live in every draw.
All inputs are finite; a program needn't handle non-finite values.
Results may differ from the reference program's by a relative error of at most 0.0003.
Values sent between devices are 32-bit elements; how exact they have to be, the bound alone decides.
No kernel may reach another device: no remote copies, remote signals or barrier semaphores. Data moves between devices by JAX's collectives and lax.ppermute only.
A program may use at most 128 MiB of HBM per device.

```python
import jax
import jax.numpy as jnp
from jax import lax

DE = 512
FT = 256
BLK = 128
LAYERS = 3
EB = 16
P_SIZE = 64
GRID = 4
TS = 4
CLUSTERS = 64


def draw_reverse(key, part):
    keys = jax.random.split(jax.random.fold_in(key, 11), 2)
    place_perm = jax.random.permutation(keys[0], GRID).astype(jnp.int32)
    inverse_perm = jnp.zeros((GRID,), jnp.int32).at[place_perm].set(jnp.arange(GRID, dtype=jnp.int32))
    rounds = EB // 2
    round_ids = jnp.arange(rounds, dtype=jnp.int32)
    offsets = 2 * (round_ids % (GRID // 2)) + 1
    partner = inverse_perm[(offsets[None, :] - place_perm[:, None]) % GRID]
    slot_keys = jax.random.split(keys[1], GRID)
    slot_perms = jax.vmap(lambda sub_key: jax.random.permutation(sub_key, EB).astype(jnp.int32))(slot_keys)
    even_slot = slot_perms[:, 0::2]
    odd_slot = slot_perms[:, 1::2]
    partner_even = slot_perms[partner, 2 * round_ids[None, :]]
    partner_odd = slot_perms[partner, 2 * round_ids[None, :] + 1]
    values_even = partner * EB + partner_odd
    values_odd = partner * EB + partner_even
    device_ids = jnp.arange(GRID, dtype=jnp.int32)[:, None]
    result = jnp.zeros((GRID, EB), jnp.int32)
    result = result.at[device_ids, even_slot].set(values_even)
    result = result.at[device_ids, odd_slot].set(values_odd)
    return result.reshape(CLUSTERS).astype(jnp.int32)


def draw_edge_counts(key, part):
    keys = jax.random.split(jax.random.fold_in(key, 23), 3)
    counts = jax.random.randint(keys[0], (CLUSTERS,), BLK // 2, BLK + 1).astype(jnp.int32)
    first = jax.random.randint(keys[1], (), 0, CLUSTERS)
    second = (first + 1 + jax.random.randint(keys[2], (), 0, CLUSTERS - 1)) % CLUSTERS
    counts = counts.at[first].set(BLK).at[second].set(BLK // 2)
    return counts.astype(jnp.int32)


def draw_trip_count(key, part):
    keys = jax.random.split(jax.random.fold_in(key, 37), 2)
    counts = jax.random.randint(keys[0], (GRID * TS,), P_SIZE // 4, P_SIZE + 1).astype(jnp.int32)
    chosen = jax.random.randint(keys[1], (), 0, GRID * TS)
    counts = counts.at[chosen].set(P_SIZE)
    return counts.reshape(GRID, TS).astype(jnp.int32)


def touch_ends(values, stream_key, low, largest):
    place = [jax.random.randint(jax.random.fold_in(stream_key, axis), (), 0, length) for axis, length in enumerate(values.shape)]
    main_axis = values.shape.index(max(values.shape))
    beside = place[:main_axis] + [(place[main_axis] + 1) % values.shape[main_axis]] + place[main_axis + 1:]
    return values.at[tuple(place)].set(low).at[tuple(beside)].set(largest)


def shard_levels(rng, shape, pieces, smallest, top_value):
    def one(axis_at, shards_of):
        heights = jax.random.uniform(jax.random.fold_in(jax.random.fold_in(rng, 6), axis_at), (shards_of,), jnp.float32, smallest / len(pieces), top_value / len(pieces))
        return jnp.repeat(jnp.exp(heights), shape[axis_at] // shards_of).reshape((-1,) + (1,) * (len(shape) - axis_at - 1))

    loudness = one(*pieces[0])
    for cut in pieces[1:]:
        loudness = loudness * one(*cut)
    return loudness


def bell_draw(rng, shape, scale, reach, pieces=(), kind=jnp.bfloat16):
    factor_of = shard_levels(rng, shape, pieces, -0.22, 0.18) if pieces else 1.0
    values = jax.random.normal(rng, shape, jnp.float32) * scale * factor_of
    return jnp.minimum(jnp.maximum(values, -reach), reach).astype(kind)


def setup_inputs(seed: int = 0, part: int = 0) -> dict:
    key_of = jax.random.split(jax.random.key(seed), 10)
    part_keys = jax.random.split(jax.random.fold_in(key_of[9], part), 10)
    return {
        "edge_feat": bell_draw(part_keys[0], (CLUSTERS, BLK, DE), 1.0, 6.0, ((0, 4), (1, 4)), jnp.float32),
        "edge_counts": draw_edge_counts(jax.random.fold_in(jax.random.fold_in(key_of[9], part), 71), part),
        "reverse": draw_reverse(jax.random.fold_in(jax.random.fold_in(key_of[9], part), 71), part),
        "patterns": touch_ends(jax.random.randint(part_keys[3], (GRID, TS, P_SIZE, 2), 0, EB), jax.random.fold_in(part_keys[3], 1), 0, EB - 1).astype(jnp.int32),
        "trip_count": draw_trip_count(jax.random.fold_in(jax.random.fold_in(key_of[9], part), 71), part),
        "coef": bell_draw(part_keys[5], (GRID, TS, P_SIZE, BLK, BLK), (BLK * P_SIZE * TS // (2 * EB)) ** -0.5, 0.1875, ((0, 4), (1, 4)), jnp.float32),
        "down_weight": bell_draw(key_of[6], (LAYERS, DE, FT), DE ** -0.5, 0.25, (), jnp.float32),
        "up_weight": bell_draw(key_of[7], (LAYERS, FT, DE), FT ** -0.5, 0.375, (), jnp.float32),
        "dense_weight": bell_draw(key_of[8], (LAYERS, DE, DE), DE ** -0.5, 0.25, (), jnp.float32),
    }


EXACT_PRECISION = lax.Precision.HIGHEST
INV_THREE = 1.0 / 3.0 ** 0.5
INV_TWO = 1.0 / 2.0 ** 0.5


def reference(edge_feat, edge_counts, reverse, patterns, trip_count, coef, down_weight, up_weight, dense_weight):
    row_ids = jnp.arange(BLK, dtype=jnp.int32)
    valid_row_mask = (row_ids[None, :] < edge_counts[:, None]).astype(jnp.float32)[:, :, None]
    edge_features = edge_feat

    def per_group(inputs):
        group_blocks, pattern_list, live_count, coeffs = inputs
        slot_live = (jnp.arange(P_SIZE, dtype=jnp.int32)[None, :] < live_count[:, None]).astype(jnp.float32)
        flat_pattern = pattern_list.reshape(TS * P_SIZE, 2)
        flat_coeffs = coeffs.reshape(TS * P_SIZE, BLK, BLK)
        picked = jnp.take(group_blocks, flat_pattern[:, 1], axis=0)
        products = jnp.einsum('pij,pjf->pif', flat_coeffs, picked, precision=EXACT_PRECISION)
        products = products * slot_live.reshape(TS * P_SIZE)[:, None, None]
        target_hot = (flat_pattern[:, 0][None, :] == jnp.arange(EB, dtype=jnp.int32)[:, None]).astype(jnp.float32)
        return jnp.einsum('tp,pif->tif', target_hot, products, precision=EXACT_PRECISION)

    for current_layer_index in range(LAYERS):
        reduced_features = jnp.einsum('mrv,ve->mre', edge_features, down_weight[current_layer_index], precision=EXACT_PRECISION) * valid_row_mask
        grouped = reduced_features.reshape(GRID, EB, BLK, FT)
        pooled_messages = lax.map(per_group, (grouped, patterns, trip_count, coef)).reshape(CLUSTERS, BLK, FT)
        raised_features = jnp.einsum('dhi,iw->dhw', pooled_messages, up_weight[current_layer_index], precision=EXACT_PRECISION)
        reversed_feat = jnp.take(raised_features, reverse, axis=0)
        merged_features = (edge_features + raised_features + reversed_feat) * INV_THREE
        dense_output = jnp.einsum('weo,oa->wea', merged_features, dense_weight[current_layer_index], precision=EXACT_PRECISION)
        edge_features = (merged_features + jax.nn.silu(dense_output)) * INV_TWO
    return edge_features
```

```python
import functools

import jax
import jax.numpy as jnp
from jax import lax
from jax.experimental import pallas as pl
from jax.experimental.pallas import tpu as pltpu
from jax.sharding import PartitionSpec as P

INV_THREE = 1.0 / 3.0**0.5
INV_TWO = 1.0 / 2.0**0.5
F32 = jnp.float32
BF16 = jnp.bfloat16
SMEM = pl.BlockSpec(memory_space=pltpu.SMEM)
VMEM = pl.BlockSpec(memory_space=pltpu.VMEM)


def split(v):
    high = v.astype(BF16)
    return high, (v - high.astype(F32)).astype(BF16)


def dot(a, b):
    return jnp.dot(a, b, preferred_element_type=F32)


def dot3(a, high, low):
    a_high, a_low = split(a)
    return dot(a_high, high) + (dot(a_low, high) + dot(a_high, low))


def params(mib):
    return pltpu.CompilerParams(vmem_limit_bytes=mib << 20)


def call(kernel, outs, ins, mib, scratch=(), flops=0, moved=0):
    return pl.pallas_call(
        kernel,
        out_shape=outs,
        in_specs=ins,
        out_specs=jax.tree.map(lambda _: VMEM, outs),
        scratch_shapes=list(scratch),
        compiler_params=params(mib),
        cost_estimate=pl.CostEstimate(flops=flops, bytes_accessed=moved, transcendentals=0),
    )


def cells_kernel(sizes, ids, pats, live, mine, theirs, rem_hi, rem_lo, loc_hi, loc_lo, acc):
    trips, chunks, rc, clusters = sizes
    x = ids[0]
    slots = mine.shape[0]
    zero = jnp.zeros(acc.shape[1:], F32)

    def clear(q, c):
        acc[q] = zero
        return c

    lax.fori_loop(0, clusters, clear, 0)
    for half, ref in enumerate((mine, theirs)):

        def add(p, c, half=half, ref=ref):
            t, q = pats[half, 2 * p], pats[half, 2 * p + 1]
            for d in range(trips):
                td = lax.rem(x + d, trips)
                for r in range(chunks):
                    g = d * chunks + r
                    acc[q, g, t] += ref[p, td, r * rc : (r + 1) * rc, :]
            return c

        lax.fori_loop(0, jnp.minimum(live[half], slots), add, 0)
    block = clusters * rc
    width = acc.shape[-1]

    def finish(q, c):
        lanes = pl.ds(pl.multiple_of(q * width, width), width)
        for d in range(trips):
            for r in range(chunks):
                high, low = split(acc[q, d * chunks + r].reshape(block, width))
                if d:
                    rem_hi[r, (d - 1) * block : d * block, lanes] = high
                    rem_lo[r, (d - 1) * block : d * block, lanes] = low
                else:
                    loc_hi[r * block : (r + 1) * block, lanes] = high
                    loc_lo[r * block : (r + 1) * block, lanes] = low
        return c

    lax.fori_loop(0, clusters, finish, 0)


def gather_kernel(sizes, places, ids, c_hi, c_lo, *refs):
    trips, subs, chunks, rc, clusters, rows, width = sizes
    pieces, (out, x_hi, x_lo) = refs[: len(places)], refs[len(places) :]
    x, s = ids[0], ids[1]
    share = chunks * rc
    for (d, other, r), ref in zip(places, pieces):
        core = 1 - s if other else s
        at = (lax.rem(x + trips - d, trips) * subs + core) * share + r * rc
        for q in range(clusters):
            high, low = split(ref[q])
            spot = pl.ds(pl.multiple_of(q * rows + at, rc), rc)
            x_hi[spot, :] = high
            x_lo[spot, :] = low
    out[...] = dot(c_hi[...], x_hi[...]) + (dot(c_lo[...], x_hi[...]) + dot(c_hi[...], x_lo[...]))


def terms_kernel(c_hi, c_lo, x_hi, x_lo, out):
    out[...] = dot(c_hi[...], x_hi[...]) + (dot(c_lo[...], x_hi[...]) + dot(c_hi[...], x_lo[...]))


def pack_kernel(sizes, arrivals, send_src, *refs):
    clusters, rc, cap = sizes
    local, refs = refs[0], refs[1:]
    got, agg, packs = refs[:arrivals], refs[arrivals], refs[arrivals + 1 :]
    total = local[...]
    for ref in got:
        total = total + ref[...]
    agg[...] = total
    for k, pack in enumerate(packs):
        for j in range(cap):
            pack[j] = agg[send_src[(k + 1) * cap + j]]


def rows_kernel(sizes, last, recv_pos, counts, ids, *refs):
    clusters, rc, cap, steps, first_row = sizes
    feat, agg, refs = refs[0], refs[1], refs[2:]
    got, refs = refs[:steps], refs[steps:]
    up_hi, up_lo, dense_hi, dense_lo, refs = *refs[:4], refs[4:]
    if last:
        (out, held, both), down = refs, None
    else:
        down, (out, low_out, held, both) = refs[:2], refs[2:]
    for k, ref in enumerate(got):
        held[k * cap : (k + 1) * cap] = ref[...]
    for c in range(clusters):
        both[c] = agg[c] + held[recv_pos[c] - cap]
    block = clusters * rc
    lifted = dot3(both[...].reshape(block, -1), up_hi[...], up_lo[...])
    merged = (feat[...].reshape(block, -1) + lifted) * INV_THREE
    v = dot3(merged, dense_hi[...], dense_lo[...])
    result = (merged + v / (1.0 + jnp.exp(-v))) * INV_TWO
    out[...] = result.reshape(out.shape)
    if not last:
        lower(result, down, counts, ids, first_row, low_out)


def lower(feat, down, counts, ids, first_row, out):
    clusters, rc, width = out.shape
    low = dot3(feat, down[0][...], down[1][...])
    ids_at = ids[2] + first_row + lax.broadcasted_iota(jnp.int32, (rc, width), 0)
    for c in range(clusters):
        out[c] = jnp.where(ids_at < counts[c], low[c * rc : (c + 1) * rc, :], 0.0)


def down_kernel(first_row, counts, ids, feat, down_hi, down_lo, out):
    lower(feat[...].reshape(out.shape[0] * out.shape[1], -1), (down_hi, down_lo), counts, ids, first_row, out)


def local(
    edge_feat,
    edge_counts,
    reverse,
    patterns,
    trip_count,
    coef,
    down_weight,
    up_weight,
    dense_weight,
):
    clusters, share, feat_width = edge_feat.shape
    layers, _, width = down_weight.shape
    edges, trips, subs = (lax.axis_size(a) for a in ("edge", "trip", "sub"))
    e, x, s = (lax.axis_index(a) for a in ("edge", "trip", "sub"))
    rows = trips * subs * share
    cap = 2 * ((clusters // 2 + edges // 2 - 1) // (edges // 2))
    rc = 16
    chunks = share // rc
    block = clusters * rc
    depth = clusters * rows
    slots = patterns.shape[2]
    ids = jnp.stack([x, s, (x * subs + s) * share]).astype(jnp.int32)
    swap = [(0, 1), (1, 0)]

    here = jnp.arange(clusters, dtype=jnp.int32)
    mine = lax.dynamic_slice_in_dim(reverse, e * clusters, clusters)
    to = mine // clusters
    earlier = (to[:, None] == to[None, :]) & (here[None, :] < here[:, None])
    send_pos = (to ^ e) * cap + jnp.sum(earlier.astype(jnp.int32), axis=1)
    places = jnp.arange(edges * cap, dtype=jnp.int32)
    send_src = jnp.sum(jnp.where(places[:, None] == send_pos[None, :], here[None, :], 0), axis=1)
    everyone = jnp.arange(reverse.shape[0], dtype=jnp.int32)
    before = (
        (everyone[None, :] // clusters == to[:, None])
        & (everyone[None, :] < mine[:, None])
        & ((reverse // clusters)[None, :] == e)
    )
    recv_pos = (to ^ e) * cap + jnp.sum(before.astype(jnp.int32), axis=1)

    def parts(w):
        high = lax.reduce_precision(w, 8, 7)
        return high.astype(BF16), (w - high).astype(BF16)

    down_hi, down_lo = parts(down_weight)
    up_hi, up_lo = parts(up_weight)
    dense_hi, dense_lo = parts(dense_weight)

    feats = [edge_feat[:, r * rc : (r + 1) * rc, :] for r in range(chunks)]
    small = jax.ShapeDtypeStruct((clusters, rc, width), F32)
    big = jax.ShapeDtypeStruct((clusters, rc, feat_width), F32)
    lows = [
        call(
            functools.partial(down_kernel, r * rc),
            small,
            [SMEM, SMEM, VMEM, VMEM, VMEM],
            16,
            flops=6 * block * feat_width * width,
        )(edge_counts, ids, feats[r], down_hi[0], down_lo[0])
        for r in range(chunks)
    ]

    halves = coef[0, 0].reshape(slots, trips, subs, share, rows)
    keep = lax.dynamic_index_in_dim(halves, s, 2, keepdims=False)
    give = lax.dynamic_index_in_dim(halves, 1 - s, 2, keepdims=False)
    note = jnp.concatenate([patterns[0, 0].reshape(-1), trip_count[0, 0][None]])
    note2 = lax.ppermute(note, "sub", swap)
    give = lax.ppermute(give, "sub", swap)
    pats = jnp.stack([note[:-1], note2[:-1]])
    live = jnp.stack([note[-1], note2[-1]])
    remote = (trips - 1) * block
    rem_hi, rem_lo, loc_hi, loc_lo = call(
        functools.partial(cells_kernel, (trips, chunks, rc, clusters)),
        [jax.ShapeDtypeStruct((chunks, remote, depth), BF16)] * 2
        + [jax.ShapeDtypeStruct((chunks * block, depth), BF16)] * 2,
        [SMEM, SMEM, SMEM, VMEM, VMEM],
        40,
        scratch=[pltpu.VMEM((clusters, trips * chunks, clusters, rc, rows), F32)],
        moved=12 << 20,
    )(ids, pats, live, keep, give)

    for layer in range(layers):
        pieces, spots = [], []
        for r in range(chunks):
            pieces += [lows[r], lax.ppermute(lows[r], "sub", swap)]
            spots += [(0, 0, r), (0, 1, r)]
            for d in range(1, trips):
                far = lax.ppermute(lows[r], "trip", [(i, (i + d) % trips) for i in range(trips)])
                pieces += [far, lax.ppermute(far, "sub", swap)]
                spots += [(d, 0, r), (d, 1, r)]
        sizes = (trips, subs, chunks, rc, clusters, rows, width)
        flops = 6 * remote * depth * width
        out, x_hi, x_lo = call(
            functools.partial(gather_kernel, sizes, spots),
            [jax.ShapeDtypeStruct((remote, width), F32)] + [jax.ShapeDtypeStruct((depth, width), BF16)] * 2,
            [SMEM, VMEM, VMEM] + [VMEM] * len(pieces),
            32,
            flops=flops,
        )(ids, rem_hi[0], rem_lo[0], *pieces)
        outs = [out]
        for r in range(1, chunks):
            outs.append(
                call(terms_kernel, jax.ShapeDtypeStruct((remote, width), F32), [VMEM] * 4, 32, flops=flops)(
                    rem_hi[r], rem_lo[r], x_hi, x_lo
                )
            )
        own = call(
            terms_kernel,
            jax.ShapeDtypeStruct((chunks * block, width), F32),
            [VMEM] * 4,
            32,
            flops=6 * chunks * block * depth * width,
        )(loc_hi, loc_lo, x_hi, x_lo).reshape(chunks, clusters, rc, width)
        next_feats, next_lows = [], []
        for r in range(chunks):
            sent = outs[r].reshape(trips - 1, clusters, rc, width)
            got = [
                lax.ppermute(sent[d - 1], "trip", [(i, (i + d) % trips) for i in range(trips)])
                for d in range(1, trips)
            ]
            agg, *packs = call(
                functools.partial(pack_kernel, (clusters, rc, cap), trips - 1),
                [small] + [jax.ShapeDtypeStruct((cap, rc, width), F32)] * (edges - 1),
                [SMEM] + [VMEM] * trips,
                16,
                moved=4 << 20,
            )(send_src, own[r], *got)
            back = [
                lax.ppermute(packs[k - 1], "edge", [(i, i ^ k) for i in range(edges)]) for k in range(1, edges)
            ]
            last = layer == layers - 1
            result = call(
                functools.partial(rows_kernel, (clusters, rc, cap, edges - 1, r * rc), last),
                [big] if last else [big, small],
                [SMEM] * 3 + [VMEM] * (2 + edges - 1 + 4 + (0 if last else 2)),
                32,
                scratch=[
                    pltpu.VMEM(((edges - 1) * cap, rc, width), F32),
                    pltpu.VMEM((clusters, rc, width), F32),
                ],
                flops=6 * block * feat_width * (2 * width + feat_width),
            )(
                recv_pos,
                edge_counts,
                ids,
                feats[r],
                agg,
                *back,
                up_hi[layer],
                up_lo[layer],
                dense_hi[layer],
                dense_lo[layer],
                *(() if last else (down_hi[layer + 1], down_lo[layer + 1])),
            )
            next_feats.append(result[0])
            next_lows += result[1:]
        feats, lows = next_feats, next_lows
    return jnp.concatenate(feats, axis=1)


def solution(mesh):
    placed = (
        P(("groups", "edge"), ("trip", "sub"), None),
        P(("groups", "edge")),
        P("groups"),
        P(("groups", "edge"), ("trip", "sub"), None, None),
        P(("groups", "edge"), ("trip", "sub")),
        P(("groups", "edge"), ("trip", "sub"), None, None, None),
        P(),
        P(),
        P(),
    )
    return jax.shard_map(
        local,
        mesh=mesh,
        in_specs=placed,
        out_specs=P(("groups", "edge"), ("trip", "sub"), None),
        check_vma=False,
    )
```

```python
import functools

import jax
import jax.numpy as jnp
from jax import lax
from jax.experimental import pallas as pl
from jax.experimental.pallas import tpu as pltpu
from jax.sharding import PartitionSpec as P

INV_THREE = 1.0 / 3.0**0.5
INV_TWO = 1.0 / 2.0**0.5
F32 = jnp.float32
BF16 = jnp.bfloat16
SMEM = pl.BlockSpec(memory_space=pltpu.SMEM)
VMEM = pl.BlockSpec(memory_space=pltpu.VMEM)
ANY = pl.BlockSpec(memory_space=pl.ANY)


def split(v):
    high = v.astype(BF16)
    return high, (v - high.astype(F32)).astype(BF16)


def dot(a, b):
    return jnp.dot(a, b, preferred_element_type=F32)


def dot3(a, high, low):
    a_high, a_low = split(a)
    return dot(a_high, high) + (dot(a_low, high) + dot(a_high, low))


def call(kernel, outs, ins, mib, out_specs=None, scratch=(), flops=0, moved=0, alias=None, grid=()):
    return pl.pallas_call(
        kernel,
        grid=grid,
        out_shape=outs,
        in_specs=ins,
        out_specs=jax.tree.map(lambda _: VMEM, outs) if out_specs is None else out_specs,
        scratch_shapes=list(scratch),
        input_output_aliases=alias or {},
        compiler_params=pltpu.CompilerParams(vmem_limit_bytes=mib << 20),
        cost_estimate=pl.CostEstimate(flops=flops, bytes_accessed=moved, transcendentals=0),
    )


def rows_of(clusters, start, size, width):
    return pl.BlockSpec((clusters, size, width), lambda i: (0, start // size, 0))


def add_cells(acc, d, pats, live, half, load, slots):
    def add(p, c):
        t, q = pats[half, 2 * p], pats[half, 2 * p + 1]
        acc[q, d, t] += load(p)
        return c

    lax.fori_loop(0, jnp.minimum(live[half], slots), add, 0)


def clear(acc):
    zero = jnp.zeros(acc.shape[1:], F32)

    def one(q, c):
        acc[q] = zero
        return c

    lax.fori_loop(0, acc.shape[0], one, 0)


def cells_kernel(sizes, ids, pats, live, mine, theirs, *refs):
    trips, subs, share, chunks, clusters = sizes
    outs, (buf, acc, sems) = refs[:-3], refs[-3:]
    n = len(chunks)
    rem_hi, rem_lo, loc_hi, loc_lo = (outs[i * n : (i + 1) * n] for i in range(4))
    x, s = ids[0], ids[1]
    slots, _, width = mine.shape
    copies = {}
    for half, ref in enumerate((mine, theirs)):
        for d in range(trips):
            start = pl.multiple_of((lax.rem(x + d, trips) * subs + s) * share, share)
            copies[half, d] = pltpu.make_async_copy(
                ref.at[:, pl.ds(start, share), :], buf.at[half, d], sems.at[half, d]
            )
            copies[half, d].start()
    clear(acc)
    for half in range(2):
        for d in range(trips):
            copies[half, d].wait()
            add_cells(acc, d, pats, live, half, lambda p, half=half, d=d: buf[half, d, p], slots)

    def finish(q, c):
        lanes = pl.ds(pl.multiple_of(q * width, width), width)
        for r, (off, rc) in enumerate(chunks):
            block = clusters * rc
            for d in range(trips):
                high, low = split(acc[q, d, :, off : off + rc, :].reshape(block, width))
                if d:
                    rem_hi[r][(d - 1) * block : d * block, lanes] = high
                    rem_lo[r][(d - 1) * block : d * block, lanes] = low
                else:
                    loc_hi[r][:, lanes] = high
                    loc_lo[r][:, lanes] = low
        return c

    lax.fori_loop(0, clusters, finish, 0)


def early_kernel(sizes, ids, pats, live, mine, theirs, *refs):
    subs, share, off, rc, clusters = sizes
    far, (out_hi, out_lo, buf, acc, sems) = refs[:-5], refs[-5:]
    slots, _, width = mine.shape
    start = pl.multiple_of((ids[0] * subs + ids[1]) * share + off, rc)
    copies = []
    for half, ref in enumerate((mine, theirs)):
        copies.append(pltpu.make_async_copy(ref.at[:, pl.ds(start, rc), :], buf.at[half], sems.at[half]))
        copies[-1].start()
    clear(acc)
    for i, ref in enumerate(far):
        add_cells(acc, 0, pats, live, 2 + i, lambda p, ref=ref: ref[p], slots)
    for half in range(2):
        copies[half].wait()
        add_cells(acc, 0, pats, live, half, lambda p, half=half: buf[half, p], slots)

    def finish(q, c):
        lanes = pl.ds(pl.multiple_of(q * width, width), width)
        high, low = split(acc[q, 0].reshape(clusters * rc, width))
        out_hi[:, lanes] = high
        out_lo[:, lanes] = low
        return c

    lax.fori_loop(0, clusters, finish, 0)


def terms(c_hi, c_lo, x_hi, x_lo):
    return dot(c_hi[...], x_hi[...]) + (dot(c_lo[...], x_hi[...]) + dot(c_hi[...], x_lo[...]))


def terms_kernel(c_hi, c_lo, x_hi, x_lo, out):
    out[...] = terms(c_hi, c_lo, x_hi, x_lo)


def pack(agg, send_src, cap, packs):
    for k, ref in enumerate(packs):
        for j in range(cap):
            ref[j] = agg[send_src[(k + 1) * cap + j]]


def gather_kernel(sizes, places, whole, ids, send_src, c_hi, c_lo, *refs):
    trips, subs, share, n, clusters, rows, cap = sizes
    count = len(places) * n
    pieces, (x_hi, x_lo, *outs) = refs[:count], refs[count:]
    x, s = ids[0], ids[1]
    for i, (d, other) in enumerate(places):
        at = (lax.rem(x + trips - d, trips) * subs + (1 - s if other else s)) * share
        group = pieces[i * n : (i + 1) * n]
        for q in range(clusters):
            high, low = split(jnp.concatenate([ref[q] for ref in group], axis=0))
            spot = pl.ds(pl.multiple_of(q * rows + at, share), share)
            x_hi[spot, :] = high
            x_lo[spot, :] = low
    out = terms(c_hi, c_lo, x_hi, x_lo)
    if whole:
        agg, *packs = outs
        agg[...] = out.reshape(agg.shape)
        pack(agg, send_src, cap, packs)
    else:
        outs[0][...] = out


def pack_kernel(cap, arrivals, send_src, local, *refs):
    got, agg, packs = refs[:arrivals], refs[arrivals], refs[arrivals + 1 :]
    total = local[...]
    for ref in got:
        total = total + ref[...]
    agg[...] = total
    pack(agg, send_src, cap, packs)


def rows_kernel(sizes, last, alias, recv_pos, counts, ids, *refs):
    clusters, rc, cap, steps, first_row = sizes
    feat, agg, refs = refs[0], refs[1], refs[2:]
    got, refs = refs[:steps], refs[steps:]
    up_hi, up_lo, dense_hi, dense_lo, refs = *refs[:4], refs[4:]
    if last:
        out, held, both = refs[1:] if alias else refs
    else:
        down, (out, low_out, held, both) = refs[:2], refs[2:]
    for k, ref in enumerate(got):
        held[k * cap : (k + 1) * cap] = ref[...]
    for c in range(clusters):
        both[c] = agg[c] + held[recv_pos[c] - cap]
    block = clusters * rc
    lifted = dot3(both[...].reshape(block, -1), up_hi[...], up_lo[...])
    merged = (feat[...].reshape(block, -1) + lifted) * INV_THREE
    v = dot3(merged, dense_hi[...], dense_lo[...])
    result = (merged + v / (1.0 + jnp.exp(-v))) * INV_TWO
    out[...] = result.reshape(out.shape)
    if not last:
        lower(result, down[0][...], down[1][...], counts, ids, first_row, low_out)


def lower(feat, down_hi, down_lo, counts, ids, first_row, out):
    clusters, rc, width = out.shape
    low = dot3(feat, down_hi, down_lo)
    row = ids[2] + first_row + lax.broadcasted_iota(jnp.int32, (rc, width), 0)
    for c in range(clusters):
        out[c] = jnp.where(row < counts[c], low[c * rc : (c + 1) * rc, :], 0.0)


def down_kernel(first_row, counts, ids, feat, down, out):
    high, low = split(down[...])
    block = out.shape[0] * out.shape[1]
    lower(feat[...].reshape(block, -1), high, low, counts, ids, first_row, out)


def local(
    edge_feat,
    edge_counts,
    reverse,
    patterns,
    trip_count,
    coef,
    down_weight,
    up_weight,
    dense_weight,
):
    clusters, share, feat_width = edge_feat.shape
    layers, _, width = down_weight.shape
    edges, trips, subs = (lax.axis_size(a) for a in ("edge", "trip", "sub"))
    e, x, s = (lax.axis_index(a) for a in ("edge", "trip", "sub"))
    rows = trips * subs * share
    cap = 2 * ((clusters // 2 + edges // 2 - 1) // (edges // 2))
    half_share = share // 2
    chunks = [(0, half_share)] + [(half_share + i, 8) for i in range(0, half_share, 8)]
    n = len(chunks)
    depth = clusters * rows
    slots = patterns.shape[2]
    swap = [(0, 1), (1, 0)]

    def turn(d):
        return [(i, (i + d) % trips) for i in range(trips)]

    ids = jnp.stack([x, s, (x * subs + s) * share]).astype(jnp.int32)
    coef = coef.reshape(coef.shape[2:])
    coef2 = lax.ppermute(coef, "sub", swap)

    def small(rc):
        return jax.ShapeDtypeStruct((clusters, rc, width), F32)

    def big(rc):
        return jax.ShapeDtypeStruct((clusters, rc, feat_width), F32)

    lows = [
        call(
            functools.partial(down_kernel, off),
            small(rc),
            [
                SMEM,
                SMEM,
                rows_of(clusters, off, rc, feat_width),
                pl.BlockSpec((None, feat_width, width), lambda i: (0, 0, 0)),
            ],
            16,
            flops=6 * clusters * rc * feat_width * width,
            grid=(1,),
            out_specs=pl.BlockSpec((clusters, rc, width), lambda i: (0, 0, 0)),
        )(edge_counts, ids, edge_feat, down_weight)
        for off, rc in chunks
    ]
    (down_weight, up_weight, dense_weight, reverse, patterns, trip_count, *lows) = lax.optimization_barrier(
        (down_weight, up_weight, dense_weight, reverse, patterns, trip_count, *lows)
    )

    note = jnp.concatenate([patterns.reshape(-1), trip_count.reshape(-1)])
    note = jnp.stack([note, lax.ppermute(note, "sub", swap)])
    notes = jnp.concatenate([note] + [lax.ppermute(note, "trip", turn(d)) for d in range(1, trips)])
    pats, live = notes[:, :-1], notes[:, -1]

    here = jnp.arange(clusters, dtype=jnp.int32)
    mine = lax.dynamic_slice_in_dim(reverse, e * clusters, clusters)
    to = mine // clusters
    earlier = (to[:, None] == to[None, :]) & (here[None, :] < here[:, None])
    send_pos = (to ^ e) * cap + jnp.sum(earlier.astype(jnp.int32), axis=1)
    places = jnp.arange(edges * cap, dtype=jnp.int32)
    send_src = jnp.sum(jnp.where(places[:, None] == send_pos[None, :], here[None, :], 0), axis=1)
    everyone = jnp.arange(reverse.shape[0], dtype=jnp.int32)
    before = (
        (everyone[None, :] // clusters == to[:, None])
        & (everyone[None, :] < mine[:, None])
        & ((reverse // clusters)[None, :] == e)
    )
    recv_pos = (to ^ e) * cap + jnp.sum(before.astype(jnp.int32), axis=1)

    def parts(w):
        high = lax.reduce_precision(w, 8, 7)
        return high.astype(BF16), (w - high).astype(BF16)

    down = [parts(down_weight[i]) for i in range(1, layers)]
    up = [parts(up_weight[i]) for i in range(layers)]
    dense = [parts(dense_weight[i]) for i in range(layers)]

    cells = call(
        functools.partial(cells_kernel, (trips, subs, share, chunks, clusters)),
        [jax.ShapeDtypeStruct(((trips - 1) * clusters * rc, depth), BF16) for _, rc in chunks] * 2
        + [jax.ShapeDtypeStruct((clusters * rc, depth), BF16) for _, rc in chunks] * 2,
        [SMEM, SMEM, SMEM, ANY, ANY],
        40,
        scratch=[
            pltpu.VMEM((2, trips, slots, share, rows), F32),
            pltpu.VMEM((clusters, trips, clusters, share, rows), F32),
            pltpu.SemaphoreType.DMA((2, trips)),
        ],
        moved=12 << 20,
    )(ids, pats[:2], live[:2], coef, coef2)
    rem_hi, rem_lo, loc_hi, loc_lo = (cells[i * n : (i + 1) * n] for i in range(4))

    feats, first = None, None
    for layer in range(layers):
        last = layer == layers - 1
        places = [(d, other) for d in range(trips) for other in range(2)]
        pieces = {}
        for r in range(n):
            for d in range(trips):
                far = lax.ppermute(lows[r], "trip", turn(d)) if d else lows[r]
                pieces[d, 0, r] = far
                pieces[d, 1, r] = lax.ppermute(far, "sub", swap)
        inputs = [pieces[d, other, r] for d, other in places for r in range(n)]
        whole = layer > 0
        order = list(range(n)) if whole else [1, 0, *range(2, n)]
        lead = order[0]
        lead_rc = chunks[lead][1]
        c_hi, c_lo = first if whole else (rem_hi[lead], rem_lo[lead])
        if whole:
            outs = [small(lead_rc)] + [jax.ShapeDtypeStruct((cap, lead_rc, width), F32)] * (edges - 1)
        else:
            outs = [jax.ShapeDtypeStruct(((trips - 1) * clusters * lead_rc, width), F32)]
        x_hi, x_lo, *outs = call(
            functools.partial(gather_kernel, (trips, subs, share, n, clusters, rows, cap), places, whole),
            [jax.ShapeDtypeStruct((depth, width), BF16)] * 2 + outs,
            [SMEM, SMEM, VMEM, VMEM] + [VMEM] * len(inputs),
            32,
            flops=6 * c_hi.shape[0] * depth * width,
        )(ids, send_src, c_hi, c_lo, *inputs)

        def product(high, low, x_hi=x_hi, x_lo=x_lo):
            return call(
                terms_kernel,
                jax.ShapeDtypeStruct((high.shape[0], width), F32),
                [VMEM] * 4,
                32,
                flops=6 * high.shape[0] * depth * width,
            )(high, low, x_hi, x_lo)

        summed = order[1:] if whole else order
        sent = {r: outs[0] if r == lead and not whole else product(rem_hi[r], rem_lo[r]) for r in summed}
        got = {}
        for r in summed:
            block = clusters * chunks[r][1]
            got[r] = [
                lax.ppermute(
                    sent[r][(d - 1) * block : d * block].reshape(clusters, -1, width), "trip", turn(d)
                )
                for d in range(1, trips)
            ]
        if layer == 0:
            off, rc = chunks[0]
            base, got[summed[-1]] = lax.optimization_barrier((ids, got[summed[-1]]))
            far = []
            for d in range(1, trips):
                for other in range(2):
                    core = 1 - base[1] if other else base[1]
                    start = (lax.rem(base[0] + d, trips) * subs + core) * share + off
                    part = lax.dynamic_slice_in_dim(coef, start, rc, 1)
                    perm = [
                        (i * subs + j, (i + d) % trips * subs + (j ^ other)) for i in range(trips) for j in range(subs)
                    ]
                    far.append(lax.ppermute(part, ("trip", "sub"), perm))
            first = call(
                functools.partial(early_kernel, (subs, share, off, rc, clusters)),
                [jax.ShapeDtypeStruct((clusters * rc, depth), BF16)] * 2,
                [SMEM, SMEM, SMEM, ANY, ANY] + [VMEM] * len(far),
                40,
                scratch=[
                    pltpu.VMEM((2, slots, rc, rows), F32),
                    pltpu.VMEM((clusters, 1, clusters, rc, rows), F32),
                    pltpu.SemaphoreType.DMA((2,)),
                ],
                moved=6 << 20,
            )(ids, pats, live, coef, coef2, *far)
        next_feats, next_lows = [None] * n, [None] * n
        result = None
        for r in order:
            off, rc = chunks[r]
            block = clusters * rc
            if r in summed:
                own = product(loc_hi[r], loc_lo[r]).reshape(clusters, rc, width)
                agg, *packs = call(
                    functools.partial(pack_kernel, cap, trips - 1),
                    [small(rc)] + [jax.ShapeDtypeStruct((cap, rc, width), F32)] * (edges - 1),
                    [SMEM] + [VMEM] * trips,
                    16,
                    moved=4 << 20,
                )(send_src, own, *got[r])
            else:
                agg, *packs = outs
            back = [None] * (edges - 1)
            for k in range(edges - 1, 0, -1):
                back[k - 1] = lax.ppermute(packs[k - 1], "edge", [(i, i ^ k) for i in range(edges)])
            alias = last and result is not None
            feat, feat_spec = (
                (edge_feat, rows_of(clusters, off, rc, feat_width))
                if layer == 0
                else (feats[r], pl.BlockSpec((clusters, rc, feat_width), lambda i: (0, 0, 0)))
            )
            extra = ([result] if alias else []) if last else list(down[layer])
            before_extra = 3 + 2 + (edges - 1) + 4
            result = call(
                functools.partial(rows_kernel, (clusters, rc, cap, edges - 1, off), last, alias),
                big(share) if last else [big(rc), small(rc)],
                [SMEM] * 3
                + [feat_spec]
                + [VMEM] * (1 + edges - 1 + 4)
                + ([ANY] * len(extra) if last else [VMEM] * len(extra)),
                32,
                grid=(1,),
                out_specs=rows_of(clusters, off, rc, feat_width) if last else [VMEM, VMEM],
                scratch=[
                    pltpu.VMEM(((edges - 1) * cap, rc, width), F32),
                    pltpu.VMEM((clusters, rc, width), F32),
                ],
                flops=6 * block * feat_width * (2 * width + feat_width),
                alias={before_extra: 0} if alias else None,
            )(recv_pos, edge_counts, ids, feat, agg, *back, *up[layer], *dense[layer], *extra)
            if not last:
                next_feats[r], next_lows[r] = result
        feats, lows = next_feats, next_lows
    return result


def solution(mesh):
    placed = (
        P(("groups", "edge"), ("trip", "sub"), None),
        P(("groups", "edge")),
        P("groups"),
        P(("groups", "edge"), ("trip", "sub"), None, None),
        P(("groups", "edge"), ("trip", "sub")),
        P(("groups", "edge"), ("trip", "sub"), None, None, None),
        P(),
        P(),
        P(),
    )
    return jax.shard_map(
        local,
        mesh=mesh,
        in_specs=placed,
        out_specs=P(("groups", "edge"), ("trip", "sub"), None),
        check_vma=False,
    )
```

```python
import functools

import jax
import jax.numpy as jnp
from jax import lax
from jax.experimental import pallas as pl
from jax.experimental.pallas import tpu as pltpu
from jax.sharding import PartitionSpec as P

INV_THREE = 1.0 / 3.0**0.5
INV_TWO = 1.0 / 2.0**0.5
F32 = jnp.float32
BF16 = jnp.bfloat16
SMEM = pl.BlockSpec(memory_space=pltpu.SMEM)
VMEM = pl.BlockSpec(memory_space=pltpu.VMEM)
ANY = pl.BlockSpec(memory_space=pl.ANY)
HBM = pl.BlockSpec(memory_space=pltpu.HBM)


def split(v):
    high = v.astype(BF16)
    return high, (v - high.astype(F32)).astype(BF16)


def dot(a, b):
    return jnp.dot(a, b, preferred_element_type=F32)


def dot3(a, high, low):
    rows = a.shape[0]
    a_high, a_low = split(a)
    both = dot(jnp.concatenate([a_high, a_low], axis=0), high)
    return both[:rows] + (both[rows:] + dot(a_high, low))


def call(kernel, outs, ins, mib, out_specs=None, scratch=(), flops=0, moved=0, alias=None, grid=()):
    return pl.pallas_call(
        kernel,
        grid=grid,
        out_shape=outs,
        in_specs=ins,
        out_specs=jax.tree.map(lambda _: VMEM, outs) if out_specs is None else out_specs,
        scratch_shapes=list(scratch),
        input_output_aliases=alias or {},
        compiler_params=pltpu.CompilerParams(vmem_limit_bytes=mib << 20),
        cost_estimate=pl.CostEstimate(flops=flops, bytes_accessed=moved, transcendentals=0),
    )


def rows_of(clusters, start, size, width):
    return pl.BlockSpec((clusters, size, width), lambda i: (0, start // size, 0))


def add_cells(acc, d, pats, live, half, load, slots):
    def add(p, c):
        t, q = pats[half, 2 * p], pats[half, 2 * p + 1]
        acc[q, d, t] += load(p)
        return c

    lax.fori_loop(0, jnp.minimum(live[half], slots), add, 0)


def clear(acc):
    zero = jnp.zeros(acc.shape[1:], F32)

    def one(q, c):
        acc[q] = zero
        return c

    lax.fori_loop(0, acc.shape[0], one, 0)


def cells_kernel(sizes, ids, pats, live, mine, theirs, *refs):
    trips, subs, share, chunks, clusters = sizes
    outs, (buf, acc, sems) = refs[:-3], refs[-3:]
    rem, own = outs[: len(chunks)], outs[len(chunks) :]
    x, s = ids[0], ids[1]
    slots, _, width = mine.shape
    copies = {}
    for half, ref in enumerate((mine, theirs)):
        for d in range(trips):
            start = pl.multiple_of((lax.rem(x + d, trips) * subs + s) * share, share)
            copies[half, d] = pltpu.make_async_copy(
                ref.at[:, pl.ds(start, share), :], buf.at[half, d], sems.at[half, d]
            )
            copies[half, d].start()
    clear(acc)
    for half in range(2):
        for d in range(trips):
            copies[half, d].wait()
            add_cells(acc, d, pats, live, half, lambda p, half=half, d=d: buf[half, d, p], slots)

    def finish(q, c):
        lanes = pl.ds(pl.multiple_of(q * width, width), width)
        for r, (off, rc) in enumerate(chunks):
            block = clusters * rc
            for d in range(trips):
                high, low = split(acc[q, d, :, off : off + rc, :].reshape(block, width))
                ref, at, lows = (rem[r], (d - 1) * block, (trips - 1) * block) if d else (own[r], 0, block)
                ref[at : at + block, lanes] = high
                ref[lows + at : lows + at + block, lanes] = low
        return c

    lax.fori_loop(0, clusters, finish, 0)


def early_kernel(sizes, ids, pats, live, mine, theirs, *refs):
    subs, share, off, rc, clusters = sizes
    far, (out, buf, acc, sems) = refs[:-4], refs[-4:]
    slots, _, width = mine.shape
    start = pl.multiple_of((ids[0] * subs + ids[1]) * share + off, rc)
    copies = []
    for half, ref in enumerate((mine, theirs)):
        copies.append(pltpu.make_async_copy(ref.at[:, pl.ds(start, rc), :], buf.at[half], sems.at[half]))
        copies[-1].start()
    clear(acc)
    for i, ref in enumerate(far):
        add_cells(acc, 0, pats, live, 2 + i, lambda p, ref=ref: ref[p], slots)
    for half in range(2):
        copies[half].wait()
        add_cells(acc, 0, pats, live, half, lambda p, half=half: buf[half, p], slots)

    def finish(q, c):
        lanes = pl.ds(pl.multiple_of(q * width, width), width)
        high, low = split(acc[q, 0].reshape(clusters * rc, width))
        out[: clusters * rc, lanes] = high
        out[clusters * rc :, lanes] = low
        return c

    lax.fori_loop(0, clusters, finish, 0)


def terms(cells, x_hi, x_lo):
    rows = cells.shape[0] // 2
    both = dot(cells[...], x_hi[...])
    return both[:rows] + (both[rows:] + dot(cells[:rows], x_lo[...]))


def terms_kernel(x_hi, x_lo, *refs):
    cells, out = refs[:-1], refs[-1]
    at = 0
    for ref in cells:
        rows = ref.shape[0] // 2
        out[at : at + rows] = terms(ref, x_hi, x_lo)
        at += rows


def pack(agg, send_src, cap, packs):
    for k, ref in enumerate(packs):
        for j in range(cap):
            ref[j] = agg[send_src[(k + 1) * cap + j]]


def gather_kernel(sizes, places, whole, ids, send_src, cells, *refs):
    trips, subs, share, n, clusters, rows, cap = sizes
    count = len(places) * n
    pieces, (x_hi, x_lo, *outs) = refs[:count], refs[count:]
    x, s = ids[0], ids[1]
    for i, (d, other) in enumerate(places):
        at = (lax.rem(x + trips - d, trips) * subs + (1 - s if other else s)) * share
        group = pieces[i * n : (i + 1) * n]
        for q in range(clusters):
            high, low = split(jnp.concatenate([ref[q] for ref in group], axis=0))
            spot = pl.ds(pl.multiple_of(q * rows + at, share), share)
            x_hi[spot, :] = high
            x_lo[spot, :] = low
    out = terms(cells, x_hi, x_lo)
    if whole:
        agg, *packs = outs
        agg[...] = out.reshape(agg.shape)
        pack(agg, send_src, cap, packs)
    else:
        outs[0][...] = out


def pack_kernel(cap, arrivals, send_src, local, *refs):
    got, outs = refs[:arrivals], refs[arrivals:]
    count = local.shape[0]
    each = len(outs) // count
    for i in range(count):
        agg, packs = outs[i * each], outs[i * each + 1 : (i + 1) * each]
        total = local[i]
        for ref in got:
            total = total + ref[i]
        agg[...] = total
        pack(agg, send_src, cap, packs)


def rows_kernel(sizes, last, unread, recv_pos, counts, ids, *refs):
    clusters, rc, cap, steps, first_row = sizes
    refs = refs[unread:]
    feat, agg, refs = refs[0], refs[1], refs[2:]
    got, refs = refs[:steps], refs[steps:]
    up_hi, up_lo, dense_hi, dense_lo, refs = *refs[:4], refs[4:]
    if last:
        out, held, both = refs
    else:
        down, (out, low_out, held, both) = refs[:2], refs[2:]
    for k, ref in enumerate(got):
        held[k * cap : (k + 1) * cap] = ref[...]
    for c in range(clusters):
        both[c] = agg[c] + held[recv_pos[c] - cap]
    block = clusters * rc
    lifted = dot3(both[...].reshape(block, -1), up_hi[...], up_lo[...])
    merged = (feat[...].reshape(block, -1) + lifted) * INV_THREE
    v = dot3(merged, dense_hi[...], dense_lo[...])
    result = (merged + v / (1.0 + jnp.exp(-v))) * INV_TWO
    out[...] = result.reshape(out.shape)
    if not last:
        lower(result, down[0][...], down[1][...], counts, ids, first_row, low_out)


def lower(feat, down_hi, down_lo, counts, ids, first_row, out):
    clusters, rc, width = out.shape
    low = dot3(feat, down_hi, down_lo)
    row = ids[2] + first_row + lax.broadcasted_iota(jnp.int32, (rc, width), 0)
    for c in range(clusters):
        out[c] = jnp.where(row < counts[c], low[c * rc : (c + 1) * rc, :], 0.0)


def down_kernel(chunks, counts, ids, feat, down, *refs):
    outs, (rows, weight, sems) = refs[:-3], refs[-3:]
    start, size = chunks[0][0], rows.shape[1]
    copies = [
        pltpu.make_async_copy(feat.at[:, start : start + size, :], rows, sems.at[0]),
        pltpu.make_async_copy(down.at[0], weight, sems.at[1]),
    ]
    for copy in copies:
        copy.start()
    copies[1].wait()
    high, low = split(weight[...])
    copies[0].wait()
    for (off, rc), out in zip(chunks, outs):
        part = rows[:, off - start : off - start + rc, :].reshape(out.shape[0] * rc, -1)
        lower(part, high, low, counts, ids, off, out)


def local(
    edge_feat,
    edge_counts,
    reverse,
    patterns,
    trip_count,
    coef,
    down_weight,
    up_weight,
    dense_weight,
):
    clusters, share, feat_width = edge_feat.shape
    layers, _, width = down_weight.shape
    edges, trips, subs = (lax.axis_size(a) for a in ("edge", "trip", "sub"))
    e, x, s = (lax.axis_index(a) for a in ("edge", "trip", "sub"))
    rows = trips * subs * share
    cap = 2 * ((clusters // 2 + edges // 2 - 1) // (edges // 2))
    half_share = share // 2
    chunks = [(0, half_share), (half_share, half_share)]
    n = len(chunks)
    depth = clusters * rows
    slots = patterns.shape[2]
    swap = [(0, 1), (1, 0)]

    def turn(d):
        return [(i, (i + d) % trips) for i in range(trips)]

    ids = jnp.stack([x, s, (x * subs + s) * share]).astype(jnp.int32)
    coef = coef.reshape(coef.shape[2:])
    coef2 = lax.ppermute(coef, "sub", swap)

    def small(rc):
        return jax.ShapeDtypeStruct((clusters, rc, width), F32)

    def big(rc):
        return jax.ShapeDtypeStruct((clusters, rc, feat_width), F32)

    lows = []
    for group in ([0], list(range(1, n))):
        lows += call(
            functools.partial(down_kernel, [chunks[r] for r in group]),
            [small(chunks[r][1]) for r in group],
            [SMEM, SMEM, HBM, HBM],
            60,
            flops=6 * clusters * half_share * feat_width * width,
            scratch=[
                pltpu.VMEM((clusters, half_share, feat_width), F32),
                pltpu.VMEM((feat_width, width), F32),
                pltpu.SemaphoreType.DMA((2,)),
            ],
        )(edge_counts, ids, edge_feat, down_weight)
    (down_weight, up_weight, dense_weight, reverse, patterns, trip_count, *lows) = lax.optimization_barrier(
        (down_weight, up_weight, dense_weight, reverse, patterns, trip_count, *lows)
    )

    note = jnp.concatenate([patterns.reshape(-1), trip_count.reshape(-1)])
    note = jnp.stack([note, lax.ppermute(note, "sub", swap)])
    here = jnp.arange(clusters, dtype=jnp.int32)
    mine = lax.dynamic_slice_in_dim(reverse, e * clusters, clusters)
    to = mine // clusters
    earlier = (to[:, None] == to[None, :]) & (here[None, :] < here[:, None])
    send_pos = (to ^ e) * cap + jnp.sum(earlier.astype(jnp.int32), axis=1)
    places = jnp.arange(edges * cap, dtype=jnp.int32)
    send_src = jnp.sum(jnp.where(places[:, None] == send_pos[None, :], here[None, :], 0), axis=1)
    everyone = jnp.arange(reverse.shape[0], dtype=jnp.int32)
    before = (
        (everyone[None, :] // clusters == to[:, None])
        & (everyone[None, :] < mine[:, None])
        & ((reverse // clusters)[None, :] == e)
    )
    recv_pos = (to ^ e) * cap + jnp.sum(before.astype(jnp.int32), axis=1)

    def parts(w):
        high = lax.reduce_precision(w, 8, 7)
        return high.astype(BF16), (w - high).astype(BF16)

    down = [parts(down_weight[i]) for i in range(1, layers)]
    up = [parts(up_weight[i]) for i in range(layers)]
    dense = [parts(dense_weight[i]) for i in range(layers)]

    cells = call(
        functools.partial(cells_kernel, (trips, subs, share, chunks, clusters)),
        [jax.ShapeDtypeStruct((2 * (trips - 1) * clusters * rc, depth), BF16) for _, rc in chunks]
        + [jax.ShapeDtypeStruct((2 * clusters * rc, depth), BF16) for _, rc in chunks],
        [SMEM, SMEM, SMEM, HBM, HBM],
        58,
        scratch=[
            pltpu.VMEM((2, trips, slots, share, rows), F32),
            pltpu.VMEM((clusters, trips, clusters, share, rows), F32),
            pltpu.SemaphoreType.DMA((2, trips)),
        ],
        moved=12 << 20,
    )(ids, note[:, :-1], note[:, -1], coef, coef2)
    cells = list(cells)

    feats, first = None, None
    for layer in range(layers):
        last = layer == layers - 1
        places = [(d, other) for d in range(trips) for other in range(2)]
        pieces = {}
        for r in range(n):
            for d in range(trips):
                far = lax.ppermute(lows[r], "trip", turn(d)) if d else lows[r]
                if layer == 0 and d:
                    far, cells[0] = lax.optimization_barrier((far, cells[0]))
                pieces[d, 0, r] = far
                pieces[d, 1, r] = lax.ppermute(far, "sub", swap)
        inputs = [pieces[d, other, r] for d, other in places for r in range(n)]
        remote, near = cells[:n], cells[n:]
        whole = layer > 0
        groups = [list(range(1, n))] if whole else [[1], [0], *[[r] for r in range(2, n)]]
        order = [0] * whole + [r for group in groups for r in group]
        lead_rc = chunks[order[0]][1]
        lead = first if whole else remote[order[0]]
        if whole:
            outs = [small(lead_rc)] + [jax.ShapeDtypeStruct((cap, lead_rc, width), F32)] * (edges - 1)
        else:
            outs = [jax.ShapeDtypeStruct((lead.shape[0] // 2, width), F32)]
        x_hi, x_lo, *outs = call(
            functools.partial(gather_kernel, (trips, subs, share, n, clusters, rows, cap), places, whole),
            [jax.ShapeDtypeStruct((depth, width), BF16)] * 2 + outs,
            [SMEM, SMEM, VMEM] + [VMEM] * len(inputs),
            32,
            flops=3 * lead.shape[0] * depth * width,
        )(ids, send_src, lead, *inputs)

        def product(group, x_hi=x_hi, x_lo=x_lo):
            size = sum(c.shape[0] // 2 for c in group)
            return call(
                terms_kernel,
                jax.ShapeDtypeStruct((size, width), F32),
                [VMEM] * (2 + len(group)),
                32,
                flops=6 * size * depth * width,
            )(x_hi, x_lo, *group)

        aggs, packs = {}, {}
        if whole:
            aggs[0], *packs[0] = outs
        sums = []
        for i, group in enumerate(groups):
            rc = chunks[group[0]][1]
            sent = outs[0] if not whole and i == 0 else product([remote[r] for r in group])
            sent = sent.reshape(len(group), trips - 1, clusters, rc, width)
            sums.append([lax.ppermute(sent[:, d - 1], "trip", turn(d)) for d in range(1, trips)])
        if layer == 0:
            off, rc = chunks[0]
            base, sums[-1] = lax.optimization_barrier((ids, sums[-1]))
            marks = jnp.pad(note[0].astype(F32), (0, rc * rows - note.shape[1])).reshape(1, rc, rows)
            far = []
            for d in range(1, trips):
                for other in range(2):
                    core = 1 - base[1] if other else base[1]
                    start = (lax.rem(base[0] + d, trips) * subs + core) * share + off
                    part = jnp.concatenate([lax.dynamic_slice_in_dim(coef, start, rc, 1), marks])
                    perm = [
                        (i * subs + j, (i + d) % trips * subs + (j ^ other)) for i in range(trips) for j in range(subs)
                    ]
                    far.append(lax.ppermute(part, ("trip", "sub"), perm))
            notes = jnp.stack([part[slots].reshape(-1)[: note.shape[1]].astype(jnp.int32) for part in far])
            notes = jnp.concatenate([note, notes])
            first = call(
                functools.partial(early_kernel, (subs, share, off, rc, clusters)),
                jax.ShapeDtypeStruct((2 * clusters * rc, depth), BF16),
                [SMEM, SMEM, SMEM, HBM, HBM] + [VMEM] * len(far),
                40,
                scratch=[
                    pltpu.VMEM((2, slots, rc, rows), F32),
                    pltpu.VMEM((clusters, 1, clusters, rc, rows), F32),
                    pltpu.SemaphoreType.DMA((2,)),
                ],
                moved=6 << 20,
            )(ids, notes[:, :-1], notes[:, -1], coef, coef2, *far)
        for group, got in zip(groups, sums):
            rc = chunks[group[0]][1]
            own = product([near[r] for r in group]).reshape(len(group), clusters, rc, width)
            packed = call(
                functools.partial(pack_kernel, cap, trips - 1),
                ([small(rc)] + [jax.ShapeDtypeStruct((cap, rc, width), F32)] * (edges - 1)) * len(group),
                [SMEM] + [VMEM] * trips,
                16,
                moved=4 << 20,
            )(send_src, own, *got)
            for i, r in enumerate(group):
                aggs[r], *packs[r] = packed[i * edges : (i + 1) * edges]
        next_feats, next_lows = [None] * n, [None] * n
        result = None
        for i, r in enumerate(order):
            off, rc = chunks[r]
            back = [None] * (edges - 1)
            for k in range(edges - 1, 0, -1):
                back[k - 1] = lax.ppermute(packs[r][k - 1], "edge", [(i, i ^ k) for i in range(edges)])
            feat, feat_spec = (
                (edge_feat, rows_of(clusters, off, rc, feat_width))
                if layer == 0
                else (feats[r], pl.BlockSpec((clusters, rc, feat_width), lambda i: (0, 0, 0)))
            )
            ahead = [packs[later][0] for later in order[i + 1 :]]
            if layer == 0 and i == n - 1:
                ahead.append(first)
            alias = {}
            if last and result is not None:
                alias = {3 + len(ahead): 0}
                ahead.append(result)
            extra = [] if last else down[layer]
            result = call(
                functools.partial(rows_kernel, (clusters, rc, cap, edges - 1, off), last, len(ahead)),
                big(share) if last else [big(rc), small(rc)],
                [SMEM] * 3
                + [ANY] * len(ahead)
                + [feat_spec]
                + [VMEM] * (1 + edges - 1 + 4 + len(extra)),
                32,
                grid=(1,),
                out_specs=rows_of(clusters, off, rc, feat_width) if last else [VMEM, VMEM],
                scratch=[
                    pltpu.VMEM(((edges - 1) * cap, rc, width), F32),
                    pltpu.VMEM((clusters, rc, width), F32),
                ],
                flops=6 * clusters * rc * feat_width * (2 * width + feat_width),
                alias=alias,
            )(recv_pos, edge_counts, ids, *ahead, feat, aggs[r], *back, *up[layer], *dense[layer], *extra)
            if not last:
                next_feats[r], next_lows[r] = result
        feats, lows = next_feats, next_lows
    return result


def solution(mesh):
    placed = (
        P(("groups", "edge"), ("trip", "sub"), None),
        P(("groups", "edge")),
        P("groups"),
        P(("groups", "edge"), ("trip", "sub"), None, None),
        P(("groups", "edge"), ("trip", "sub")),
        P(("groups", "edge"), ("trip", "sub"), None, None, None),
        P(),
        P(),
        P(),
    )
    return jax.shard_map(
        local,
        mesh=mesh,
        in_specs=placed,
        out_specs=P(("groups", "edge"), ("trip", "sub"), None),
        check_vma=False,
    )
```

```python
import functools

import jax
import jax.numpy as jnp
from jax import lax
from jax.experimental import pallas as pl
from jax.experimental.pallas import tpu as pltpu
from jax.sharding import PartitionSpec as P

INV_THREE = 1.0 / 3.0**0.5
INV_TWO = 1.0 / 2.0**0.5
F32 = jnp.float32
BF16 = jnp.bfloat16
SMEM = pl.BlockSpec(memory_space=pltpu.SMEM)
VMEM = pl.BlockSpec(memory_space=pltpu.VMEM)
ANY = pl.BlockSpec(memory_space=pl.ANY)
HBM = pl.BlockSpec(memory_space=pltpu.HBM)


def split(v):
    high = v.astype(BF16)
    return high, (v - high.astype(F32)).astype(BF16)


def dot(a, b):
    return jnp.dot(a, b, preferred_element_type=F32)


def dot3(a, high, low):
    rows = a.shape[0]
    a_high, a_low = split(a)
    both = dot(jnp.concatenate([a_high, a_low], axis=0), high)
    return both[:rows] + (both[rows:] + dot(a_high, low))


def call(kernel, outs, ins, mib, out_specs=None, scratch=(), flops=0, moved=0, alias=None, grid=()):
    return pl.pallas_call(
        kernel,
        grid=grid,
        out_shape=outs,
        in_specs=ins,
        out_specs=jax.tree.map(lambda _: VMEM, outs) if out_specs is None else out_specs,
        scratch_shapes=list(scratch),
        input_output_aliases=alias or {},
        compiler_params=pltpu.CompilerParams(vmem_limit_bytes=mib << 20),
        cost_estimate=pl.CostEstimate(flops=flops, bytes_accessed=moved, transcendentals=0),
    )


def rows_of(clusters, start, size, width):
    return pl.BlockSpec((clusters, size, width), lambda i: (0, start // size, 0))


def add_cells(acc, d, pats, live, half, load, slots):
    def add(p, c):
        t, q = pats[half, 2 * p], pats[half, 2 * p + 1]
        acc[q, d, t] += load(p)
        return c

    lax.fori_loop(0, jnp.minimum(live[half], slots), add, 0)


def clear(acc):
    zero = jnp.zeros(acc.shape[1:], F32)

    def one(q, c):
        acc[q] = zero
        return c

    lax.fori_loop(0, acc.shape[0], one, 0)


def finish_cells(clusters, acc, counts, groups):
    width = acc.shape[-1]

    def finish(q, c):
        lanes = pl.ds(pl.multiple_of(q * width, width), width)
        for d, off, rc, ref, at in groups:
            block = clusters * rc
            alive = lax.broadcasted_iota(jnp.int32, (block, width), 1) < counts[q]
            cell = acc[q, d, :, off : off + rc, :].reshape(block, width)
            high, low = split(jnp.where(alive, cell, 0.0))
            ref[at : at + block, lanes] = high
            lows = ref.shape[0] // 2 + at
            ref[lows : lows + block, lanes] = low
        return c

    lax.fori_loop(0, clusters, finish, 0)


def near_kernel(sizes, ids, counts, pats, live, mine, theirs, *refs):
    trips, subs, share, chunks, clusters = sizes
    outs, (buf, acc, sems) = refs[:-3], refs[-3:]
    slots = mine.shape[0]
    start = pl.multiple_of((ids[0] * subs + ids[1]) * share, share)
    copies = []
    for half, ref in enumerate((mine, theirs)):
        copies.append(pltpu.make_async_copy(ref.at[:, pl.ds(start, share), :], buf.at[half], sems.at[half]))
        copies[-1].start()
    clear(acc)
    for half in range(2):
        copies[half].wait()
        add_cells(acc, 0, pats, live, half, lambda p, half=half: buf[half, p], slots)
    finish_cells(clusters, acc, counts, [(0, off, rc, outs[r], 0) for r, (off, rc) in enumerate(chunks)])


def remote_kernel(sizes, ids, counts, pats, live, marks, mine, theirs, *refs):
    trips, subs, share, chunks, clusters = sizes
    n = len(chunks)
    outs, parts, (buf, acc, sems, part_sems) = refs[:n], refs[n:-4], refs[-4:]
    x, s = ids[0], ids[1]
    slots = mine.shape[0]
    copies, part_copies = {}, []
    for half, ref in enumerate((mine, theirs)):
        for d in range(1, trips):
            start = pl.multiple_of((lax.rem(x + d, trips) * subs + s) * share, share)
            copies[half, d] = pltpu.make_async_copy(
                ref.at[:, pl.ds(start, share), :], buf.at[half, d - 1], sems.at[half, d - 1]
            )
            copies[half, d].start()
    off, rc = chunks[0]
    for i, part in enumerate(parts):
        core = 1 - s if i % 2 else s
        start = pl.multiple_of((lax.rem(x + 1 + i // 2, trips) * subs + core) * share + off, rc)
        for k, (src, at, size) in enumerate(((mine.at[:, pl.ds(start, rc), :], 0, slots), (marks, slots, 1))):
            part_copies.append(pltpu.make_async_copy(src, part.at[at : at + size], part_sems.at[i, k]))
            part_copies[-1].start()
    clear(acc)
    for half in range(2):
        for d in range(1, trips):
            copies[half, d].wait()
            add_cells(acc, d - 1, pats, live, half, lambda p, half=half, d=d: buf[half, d - 1, p], slots)
    groups = [
        (d - 1, off, rc, outs[r], (d - 1) * clusters * rc)
        for r, (off, rc) in enumerate(chunks)
        for d in range(1, trips)
    ]
    finish_cells(clusters, acc, counts, groups)
    for copy in part_copies:
        copy.wait()


def early_kernel(sizes, ids, counts, pats, live, mine, theirs, *refs):
    subs, share, off, rc, clusters = sizes
    far, (out, buf, acc, sems) = refs[:-4], refs[-4:]
    slots = mine.shape[0]
    start = pl.multiple_of((ids[0] * subs + ids[1]) * share + off, rc)
    copies = []
    for half, ref in enumerate((mine, theirs)):
        copies.append(pltpu.make_async_copy(ref.at[:, pl.ds(start, rc), :], buf.at[half], sems.at[half]))
        copies[-1].start()
    clear(acc)
    for i, ref in enumerate(far):
        add_cells(acc, 0, pats, live, 2 + i, lambda p, ref=ref: ref[p], slots)
    for half in range(2):
        copies[half].wait()
        add_cells(acc, 0, pats, live, half, lambda p, half=half: buf[half, p], slots)
    finish_cells(clusters, acc, counts, [(0, 0, rc, out, 0)])


def terms(cells, x_hi, x_lo):
    rows = cells.shape[0] // 2
    both = dot(cells[...], x_hi[...])
    return both[:rows] + (both[rows:] + dot(cells[:rows], x_lo[...]))


def terms_kernel(x_hi, x_lo, *refs):
    cells, out = refs[:-1], refs[-1]
    at = 0
    for ref in cells:
        rows = ref.shape[0] // 2
        out[at : at + rows] = terms(ref, x_hi, x_lo)
        at += rows


def pack(agg, send_src, cap, packs):
    for k, ref in enumerate(packs):
        for j in range(cap):
            ref[j] = agg[send_src[(k + 1) * cap + j]]


def gather_kernel(sizes, places, whole, ids, send_src, cells, *refs):
    trips, subs, share, n, clusters, rows, cap = sizes
    count = len(places) * n
    pieces, (x_hi, x_lo, *outs) = refs[:count], refs[count:]
    x, s = ids[0], ids[1]
    for i, (d, other) in enumerate(places):
        at = (lax.rem(x + trips - d, trips) * subs + (1 - s if other else s)) * share
        group = pieces[i * n : (i + 1) * n]
        for q in range(clusters):
            high, low = split(jnp.concatenate([ref[q] for ref in group], axis=0))
            spot = pl.ds(pl.multiple_of(q * rows + at, share), share)
            x_hi[spot, :] = high
            x_lo[spot, :] = low
    out = terms(cells, x_hi, x_lo)
    if whole:
        agg, *packs = outs
        agg[...] = out.reshape(agg.shape)
        pack(agg, send_src, cap, packs)
    else:
        outs[0][...] = out


def pack_kernel(cap, arrivals, send_src, local, *refs):
    got, outs = refs[:arrivals], refs[arrivals:]
    count = local.shape[0]
    each = len(outs) // count
    for i in range(count):
        agg, packs = outs[i * each], outs[i * each + 1 : (i + 1) * each]
        total = local[i]
        for ref in got:
            total = total + ref[i]
        agg[...] = total
        pack(agg, send_src, cap, packs)


def rows_kernel(sizes, last, unread, recv_pos, *refs):
    clusters, rc, cap, steps = sizes
    count = len(steps)
    refs = refs[unread:]
    feat, agg, refs = refs[0], refs[1], refs[2:]
    got, refs = refs[:count], refs[count:]
    up_hi, up_lo, dense_hi, dense_lo, refs = *refs[:4], refs[4:]
    if last:
        out, held, both = refs
    else:
        down, (out, low_out, held, both) = refs[:2], refs[2:]
    for k, ref in zip(steps, got):
        held[(k - 1) * cap : k * cap] = ref[...]
    for c in range(clusters):
        both[c] = agg[c] + held[recv_pos[c] - cap]
    block = clusters * rc
    lifted = dot3(both[...].reshape(block, -1), up_hi[...], up_lo[...])
    merged = (feat[...].reshape(block, -1) + lifted) * INV_THREE
    v = dot3(merged, dense_hi[...], dense_lo[...])
    result = (merged + v / (1.0 + jnp.exp(-v))) * INV_TWO
    out[...] = result.reshape(out.shape)
    if not last:
        low_out[...] = dot3(result, down[0][...], down[1][...]).reshape(low_out.shape)


def down_kernel(chunks, feat, down, *refs):
    outs, (rows, weight, sems) = refs[:-3], refs[-3:]
    copies = [pltpu.make_async_copy(down.at[0], weight, sems.at[0])]
    for r, (off, rc) in enumerate(chunks):
        part = slice(off, off + rc)
        copies.append(pltpu.make_async_copy(feat.at[:, part, :], rows.at[:, part, :], sems.at[1 + r]))
    for copy in copies:
        copy.start()
    copies[0].wait()
    high, low = split(weight[...])
    for r, (off, rc) in enumerate(chunks):
        copies[1 + r].wait()
        part = rows[:, off : off + rc, :].reshape(-1, rows.shape[-1])
        outs[r][...] = dot3(part, high, low).reshape(outs[r].shape)


def local(
    edge_feat,
    edge_counts,
    reverse,
    patterns,
    trip_count,
    coef,
    down_weight,
    up_weight,
    dense_weight,
):
    clusters, share, feat_width = edge_feat.shape
    layers, _, width = down_weight.shape
    edges, trips, subs = (lax.axis_size(a) for a in ("edge", "trip", "sub"))
    e, x, s = (lax.axis_index(a) for a in ("edge", "trip", "sub"))
    rows = trips * subs * share
    cap = 2 * ((clusters // 2 + edges // 2 - 1) // (edges // 2))
    half_share = share // 2
    chunks = [(0, half_share), (half_share, half_share)]
    n = len(chunks)
    depth = clusters * rows
    slots = patterns.shape[2]
    swap = [(0, 1), (1, 0)]

    def turn(d):
        return [(i, (i + d) % trips) for i in range(trips)]

    ids = jnp.stack([x, s]).astype(jnp.int32)
    coef = coef.reshape(coef.shape[2:])
    coef2 = lax.ppermute(coef, "sub", swap)

    def small(rc):
        return jax.ShapeDtypeStruct((clusters, rc, width), F32)

    def big(rc):
        return jax.ShapeDtypeStruct((clusters, rc, feat_width), F32)

    lows = call(
        functools.partial(down_kernel, chunks),
        [small(rc) for _, rc in chunks],
        [HBM, HBM],
        60,
        flops=6 * clusters * share * feat_width * width,
        scratch=[
            pltpu.VMEM((clusters, share, feat_width), F32),
            pltpu.VMEM((feat_width, width), F32),
            pltpu.SemaphoreType.DMA((1 + n,)),
        ],
    )(edge_feat, down_weight)
    (down_weight, up_weight, dense_weight, reverse, patterns, trip_count, *lows) = lax.optimization_barrier(
        (down_weight, up_weight, dense_weight, reverse, patterns, trip_count, *lows)
    )

    note = jnp.concatenate([patterns.reshape(-1), trip_count.reshape(-1)])
    note = jnp.stack([note, lax.ppermute(note, "sub", swap)])
    here = jnp.arange(clusters, dtype=jnp.int32)
    mine = lax.dynamic_slice_in_dim(reverse, e * clusters, clusters)
    to = mine // clusters
    earlier = (to[:, None] == to[None, :]) & (here[None, :] < here[:, None])
    send_pos = (to ^ e) * cap + jnp.sum(earlier.astype(jnp.int32), axis=1)
    places = jnp.arange(edges * cap, dtype=jnp.int32)
    send_src = jnp.sum(jnp.where(places[:, None] == send_pos[None, :], here[None, :], 0), axis=1)
    everyone = jnp.arange(reverse.shape[0], dtype=jnp.int32)
    before = (
        (everyone[None, :] // clusters == to[:, None])
        & (everyone[None, :] < mine[:, None])
        & ((reverse // clusters)[None, :] == e)
    )
    recv_pos = (to ^ e) * cap + jnp.sum(before.astype(jnp.int32), axis=1)

    def parts(w):
        high = lax.reduce_precision(w, 8, 7)
        return high.astype(BF16), (w - high).astype(BF16)

    down = [parts(down_weight[i]) for i in range(1, layers)]
    up = [parts(up_weight[i]) for i in range(layers)]
    dense = [parts(dense_weight[i]) for i in range(layers)]

    lead_rows = chunks[0][1]
    marks = jnp.pad(note[0].astype(F32), (0, lead_rows * rows - note.shape[1])).reshape(1, lead_rows, rows)
    remote = call(
        functools.partial(remote_kernel, (trips, subs, share, chunks, clusters)),
        [jax.ShapeDtypeStruct((2 * (trips - 1) * clusters * rc, depth), BF16) for _, rc in chunks]
        + [jax.ShapeDtypeStruct((slots + 1, lead_rows, rows), F32)] * (2 * (trips - 1)),
        [SMEM] * 4 + [HBM] * 3,
        40,
        scratch=[
            pltpu.VMEM((2, trips - 1, slots, share, rows), F32),
            pltpu.VMEM((clusters, trips - 1, clusters, share, rows), F32),
            pltpu.SemaphoreType.DMA((2, trips - 1)),
            pltpu.SemaphoreType.DMA((2 * (trips - 1), 2)),
        ],
        moved=12 << 20,
    )(ids, edge_counts, note[:, :-1], note[:, -1], marks, coef, coef2)
    remote, parts = list(remote[:n]), remote[n:]

    feats, first = None, None
    for layer in range(layers):
        last = layer == layers - 1
        places = [(d, other) for d in range(trips) for other in range(2)]
        pieces = {}
        for r in range(n):
            for d in range(trips):
                far = lax.ppermute(lows[r], "trip", turn(d)) if d else lows[r]
                if layer == 0 and d:
                    far, remote[0] = lax.optimization_barrier((far, remote[0]))
                pieces[d, 0, r] = far
                pieces[d, 1, r] = lax.ppermute(far, "sub", swap)
        inputs = [pieces[d, other, r] for d, other in places for r in range(n)]
        whole = layer > 0
        groups = [list(range(1, n))] if whole else [[1], [0], *[[r] for r in range(2, n)]]
        order = [0] * whole + [r for group in groups for r in group]
        lead_rc = chunks[order[0]][1]
        lead = first if whole else remote[order[0]]
        if whole:
            outs = [small(lead_rc)] + [jax.ShapeDtypeStruct((cap, lead_rc, width), F32)] * (edges - 1)
        else:
            outs = [jax.ShapeDtypeStruct((lead.shape[0] // 2, width), F32)]
        x_hi, x_lo, *outs = call(
            functools.partial(gather_kernel, (trips, subs, share, n, clusters, rows, cap), places, whole),
            [jax.ShapeDtypeStruct((depth, width), BF16)] * 2 + outs,
            [SMEM, SMEM, VMEM] + [VMEM] * len(inputs),
            32,
            flops=3 * lead.shape[0] * depth * width,
        )(ids, send_src, lead, *inputs)

        def product(group, x_hi=x_hi, x_lo=x_lo):
            size = sum(c.shape[0] // 2 for c in group)
            return call(
                terms_kernel,
                jax.ShapeDtypeStruct((size, width), F32),
                [VMEM] * (2 + len(group)),
                32,
                flops=6 * size * depth * width,
            )(x_hi, x_lo, *group)

        aggs, packs = {}, {}
        if whole:
            aggs[0], *packs[0] = outs
        sums = []
        for i, group in enumerate(groups):
            rc = chunks[group[0]][1]
            sent = outs[0] if not whole and i == 0 else product([remote[r] for r in group])
            sent = sent.reshape(len(group), trips - 1, clusters, rc, width)
            sums.append([lax.ppermute(sent[:, d - 1], "trip", turn(d)) for d in range(1, trips)])
        if layer == 0:
            near = call(
                functools.partial(near_kernel, (trips, subs, share, chunks, clusters)),
                [jax.ShapeDtypeStruct((2 * clusters * rc, depth), BF16) for _, rc in chunks],
                [SMEM] * 4 + [HBM] * 2,
                40,
                scratch=[
                    pltpu.VMEM((2, slots, share, rows), F32),
                    pltpu.VMEM((clusters, 1, clusters, share, rows), F32),
                    pltpu.SemaphoreType.DMA((2,)),
                ],
                moved=8 << 20,
            )(ids, edge_counts, note[:, :-1], note[:, -1], coef, coef2)
        for group, got in zip(groups, sums):
            rc = chunks[group[0]][1]
            own = product([near[r] for r in group]).reshape(len(group), clusters, rc, width)
            packed = call(
                functools.partial(pack_kernel, cap, trips - 1),
                ([small(rc)] + [jax.ShapeDtypeStruct((cap, rc, width), F32)] * (edges - 1)) * len(group),
                [SMEM] + [VMEM] * trips,
                16,
                moved=4 << 20,
            )(send_src, own, *got)
            for i, r in enumerate(group):
                aggs[r], *packs[r] = packed[i * edges : (i + 1) * edges]
        if layer == 0:
            off, rc = chunks[0]
            parts, packs[order[-1]] = lax.optimization_barrier((parts, packs[order[-1]]))
            far = []
            for d in range(1, trips):
                for other in range(2):
                    perm = [
                        (i * subs + j, (i + d) % trips * subs + (j ^ other)) for i in range(trips) for j in range(subs)
                    ]
                    far.append(lax.ppermute(parts[2 * (d - 1) + other], ("trip", "sub"), perm))
            notes = jnp.stack([part[slots].reshape(-1)[: note.shape[1]].astype(jnp.int32) for part in far])
            notes = jnp.concatenate([note, notes])
            first = call(
                functools.partial(early_kernel, (subs, share, off, rc, clusters)),
                jax.ShapeDtypeStruct((2 * clusters * rc, depth), BF16),
                [SMEM] * 4 + [HBM] * 2 + [VMEM] * len(far),
                40,
                scratch=[
                    pltpu.VMEM((2, slots, rc, rows), F32),
                    pltpu.VMEM((clusters, 1, clusters, rc, rows), F32),
                    pltpu.SemaphoreType.DMA((2,)),
                ],
                moved=6 << 20,
            )(ids, edge_counts, notes[:, :-1], notes[:, -1], coef, coef2, *far)
        next_feats, next_lows = [None] * n, [None] * n
        result = None
        for i, r in enumerate(order):
            off, rc = chunks[r]
            steps = list(range(edges - 1, 0, -1))
            back = [lax.ppermute(packs[r][k - 1], "edge", [(i, i ^ k) for i in range(edges)]) for k in steps]
            feat, feat_spec = (
                (edge_feat, rows_of(clusters, off, rc, feat_width))
                if layer == 0
                else (feats[r], pl.BlockSpec((clusters, rc, feat_width), lambda i: (0, 0, 0)))
            )
            ahead = [packs[later][0] for later in order[i + 1 :]]
            if layer == 0 and i == n - 1:
                ahead.append(first)
            alias = {}
            if last and result is not None:
                alias = {1 + len(ahead): 0}
                ahead.append(result)
            extra = [] if last else down[layer]
            result = call(
                functools.partial(rows_kernel, (clusters, rc, cap, steps), last, len(ahead)),
                big(share) if last else [big(rc), small(rc)],
                [SMEM]
                + [ANY] * len(ahead)
                + [feat_spec]
                + [VMEM] * (1 + edges - 1 + 4 + len(extra)),
                32,
                grid=(1,),
                out_specs=rows_of(clusters, off, rc, feat_width) if last else [VMEM, VMEM],
                scratch=[
                    pltpu.VMEM(((edges - 1) * cap, rc, width), F32),
                    pltpu.VMEM((clusters, rc, width), F32),
                ],
                flops=6 * clusters * rc * feat_width * (2 * width + feat_width),
                alias=alias,
            )(recv_pos, *ahead, feat, aggs[r], *back, *up[layer], *dense[layer], *extra)
            if not last:
                next_feats[r], next_lows[r] = result
        feats, lows = next_feats, next_lows
    return result


def solution(mesh):
    placed = (
        P(("groups", "edge"), ("trip", "sub"), None),
        P(("groups", "edge")),
        P("groups"),
        P(("groups", "edge"), ("trip", "sub"), None, None),
        P(("groups", "edge"), ("trip", "sub")),
        P(("groups", "edge"), ("trip", "sub"), None, None, None),
        P(),
        P(),
        P(),
    )
    return jax.shard_map(
        local,
        mesh=mesh,
        in_specs=placed,
        out_specs=P(("groups", "edge"), ("trip", "sub"), None),
        check_vma=False,
    )
```

```python
import functools

import jax
import jax.numpy as jnp
from jax import lax
from jax.experimental import pallas as pl
from jax.experimental.pallas import tpu as pltpu
from jax.sharding import PartitionSpec as P

INV_THREE = 1.0 / 3.0**0.5
INV_TWO = 1.0 / 2.0**0.5
F32 = jnp.float32
BF16 = jnp.bfloat16
SMEM = pl.BlockSpec(memory_space=pltpu.SMEM)
VMEM = pl.BlockSpec(memory_space=pltpu.VMEM)
ANY = pl.BlockSpec(memory_space=pl.ANY)
HBM = pl.BlockSpec(memory_space=pltpu.HBM)


def split(v):
    high = v.astype(BF16)
    return high, (v - high.astype(F32)).astype(BF16)


def dot(a, b):
    return jnp.dot(a, b, preferred_element_type=F32)


def dot3(a, high, low):
    rows = a.shape[0]
    a_high, a_low = split(a)
    both = dot(jnp.concatenate([a_high, a_low], axis=0), high)
    return both[:rows] + (both[rows:] + dot(a_high, low))


def call(kernel, outs, ins, mib, out_specs=None, scratch=(), flops=0, moved=0, alias=None, grid=()):
    return pl.pallas_call(
        kernel,
        grid=grid,
        out_shape=outs,
        in_specs=ins,
        out_specs=jax.tree.map(lambda _: VMEM, outs) if out_specs is None else out_specs,
        scratch_shapes=list(scratch),
        input_output_aliases=alias or {},
        compiler_params=pltpu.CompilerParams(vmem_limit_bytes=mib << 20),
        cost_estimate=pl.CostEstimate(flops=flops, bytes_accessed=moved, transcendentals=0),
    )


def rows_of(clusters, start, size, width):
    return pl.BlockSpec((clusters, size, width), lambda i: (0, start // size, 0))


def add_cells(acc, pats, live, half, count, slots, load):
    many = 4 if slots % 4 == 0 else 1
    alive = jnp.minimum(live[half], slots)

    def add(i, c):
        found = []
        for p in [many * i + u for u in range(many)]:
            values = [jnp.where(p < alive, load(p, d), 0.0) for d in range(count)]
            found.append((pats[half, 2 * p], pats[half, 2 * p + 1], values))
        for t, q, values in found:
            for d, value in enumerate(values):
                acc[q, d, t] += value
        return c

    lax.fori_loop(0, lax.div(alive + (many - 1), many), add, 0)


def clear(acc):
    zero = jnp.zeros(acc.shape[1:], F32)

    def one(q, c):
        acc[q] = zero
        return c

    lax.fori_loop(0, acc.shape[0], one, 0)


def finish_cells(sizes, x, acc, counts, groups):
    trips, subs, share, clusters = sizes
    width, chip = trips * subs * share, subs * share
    step = clusters // 2

    def finish(g, c):
        for d, off, rc, ref, at in groups:
            block = step * rc
            lane = lax.broadcasted_iota(jnp.int32, (block, width), 1)
            for t in range(0, clusters, step):
                cells = []
                for j in range(trips):
                    cell = acc[g * trips + j, d, t : t + step, off : off + rc, :].reshape(block, width)
                    cells.append(jnp.where(lane < counts[g * trips + j], cell, 0.0))
                bit = 1
                while bit < trips:
                    low_half = lane // chip % (2 * bit) < bit
                    for i in range(trips):
                        if not i & bit:
                            a, b = cells[i], cells[i | bit]
                            cells[i] = jnp.where(low_half, a, pltpu.roll(b, bit * chip, 1))
                            cells[i | bit] = jnp.where(low_half, pltpu.roll(a, width - bit * chip, 1), b)
                    bit *= 2
                for i, cell in enumerate(cells):
                    place = lax.rem(x + trips - i, trips) * clusters * chip + g * width
                    lanes = pl.ds(pl.multiple_of(place, width), width)
                    row = at + t * rc
                    high, low = split(cell)
                    ref[row : row + block, lanes] = high
                    row += ref.shape[0] // 2
                    ref[row : row + block, lanes] = low
        return c

    lax.fori_loop(0, clusters // trips, finish, 0)


def cells_kernel(sizes, ids, counts, pats, live, marks, mine, theirs, *refs):
    trips, subs, share, chunks, clusters = sizes
    n = len(chunks)
    near, remote, parts, (buf, acc, sems, part_sems) = refs[:n], refs[n : 2 * n], refs[2 * n : -4], refs[-4:]
    x, s = ids[0], ids[1]
    slots = mine.shape[0]
    copies, part_copies = [], []
    for half, ref in enumerate((mine, theirs)):
        for d in range(trips):
            start = pl.multiple_of((lax.rem(x + d, trips) * subs + s) * share, share)
            copies.append(
                pltpu.make_async_copy(ref.at[:, pl.ds(start, share), :], buf.at[half, d], sems.at[half, d])
            )
            copies[-1].start()
    off, rc = chunks[0]
    for i, part in enumerate(parts):
        core = 1 - s if i % 2 else s
        start = pl.multiple_of((lax.rem(x + 1 + i // 2, trips) * subs + core) * share + off, rc)
        for k, (src, at, size) in enumerate(((mine.at[:, pl.ds(start, rc), :], 0, slots), (marks, slots, 1))):
            part_copies.append(pltpu.make_async_copy(src, part.at[at : at + size], part_sems.at[i, k]))
            part_copies[-1].start()
    clear(acc)
    for half in range(2):
        for d in range(trips):
            copies[half * trips + d].wait()
        add_cells(acc, pats, live, half, trips, slots, lambda p, d, half=half: buf[half, d, p])
    groups = []
    for r, (off, rc) in enumerate(chunks):
        groups.append((0, off, rc, near[r], 0))
        groups += [(d, off, rc, remote[r], (d - 1) * clusters * rc) for d in range(1, trips)]
    finish_cells((trips, subs, share, clusters), x, acc, counts, groups)
    for copy in part_copies:
        copy.wait()


def early_kernel(sizes, ids, counts, pats, live, mine, theirs, *refs):
    trips, subs, share, off, rc, clusters = sizes
    far, (out, buf, acc, sems) = refs[:-4], refs[-4:]
    slots = mine.shape[0]
    start = pl.multiple_of((ids[0] * subs + ids[1]) * share + off, rc)
    copies = []
    for half, ref in enumerate((mine, theirs)):
        copies.append(pltpu.make_async_copy(ref.at[:, pl.ds(start, rc), :], buf.at[half], sems.at[half]))
        copies[-1].start()
    clear(acc)
    for i, ref in enumerate(far):
        add_cells(acc, pats, live, 2 + i, 1, slots, lambda p, d, ref=ref: ref[p])
    for half in range(2):
        copies[half].wait()
        add_cells(acc, pats, live, half, 1, slots, lambda p, d, half=half: buf[half, p])
    finish_cells((trips, subs, share, clusters), ids[0], acc, counts, [(0, 0, rc, out, 0)])


def terms(cells, x_hi, x_lo, first=0):
    rows = cells.shape[0] // 2
    columns = slice(first, first + x_hi.shape[0])
    both = dot(cells[:, columns], x_hi[...])
    return both[:rows] + (both[rows:] + dot(cells[:rows, columns], x_lo[...]))


def spread(s, n, pieces, x_hi, x_lo):
    clusters = pieces[0].shape[0]
    share = sum(ref.shape[1] for ref in pieces[:n])
    for i in range(0, len(pieces) // n):
        core = 1 - s if i % 2 else s
        for q in range(clusters):
            high, low = split(jnp.concatenate([ref[q] for ref in pieces[i * n : (i + 1) * n]], axis=0))
            at = (i // 2 * clusters + q) * 2 * share + core * share
            spot = pl.ds(pl.multiple_of(at, share), share)
            x_hi[spot, :] = high
            x_lo[spot, :] = low


def near_kernel(home_hi, home_lo, far_hi, far_lo, cells, out):
    out[...] = terms(cells, home_hi, home_lo) + terms(cells, far_hi, far_lo, home_hi.shape[0])


def home_kernel(n, ids, one, two, *refs):
    pieces, (x_hi, x_lo, one_out, two_out) = refs[:-4], refs[-4:]
    spread(ids[1], n, pieces, x_hi, x_lo)
    one_out[...] = terms(one, x_hi, x_lo)
    two_out[...] = terms(two, x_hi, x_lo)


def pack(agg, send_src, cap, packs):
    for k, ref in enumerate(packs):
        for j in range(cap):
            ref[j] = agg[send_src[(k + 1) * cap + j]]


def far_kernel(n, count, cap, whole, ids, send_src, one, two, one_in, two_in, *refs):
    pieces, (x_hi, x_lo, two_out, *outs) = refs[:count], refs[count:]
    first = one.shape[1] - x_hi.shape[0]
    spread(ids[1], n, pieces, x_hi, x_lo)
    out = one_in[...] + terms(one, x_hi, x_lo, first)
    two_out[...] = two_in[...] + terms(two, x_hi, x_lo, first)
    if whole:
        agg, *packs = outs
        agg[...] = out.reshape(agg.shape)
        pack(agg, send_src, cap, packs)
    else:
        outs[0][...] = out


def pack_kernel(cap, arrivals, send_src, local, *refs):
    got, (agg, *packs) = refs[:arrivals], refs[arrivals:]
    total = local[...]
    for ref in got:
        total = total + ref[...]
    agg[...] = total
    pack(agg, send_src, cap, packs)


def rows_kernel(sizes, last, unread, recv_pos, *refs):
    clusters, rc, cap, steps = sizes
    refs = refs[unread:]
    feat, agg, refs = refs[0], refs[1], refs[2:]
    got, refs = refs[: len(steps)], refs[len(steps) :]
    up_hi, up_lo, dense_hi, dense_lo, refs = *refs[:4], refs[4:]
    if last:
        out, held, both = refs
    else:
        down, (out, low_out, held, both) = refs[:2], refs[2:]
    for k, ref in zip(steps, got):
        held[(k - 1) * cap : k * cap] = ref[...]
    for c in range(clusters):
        both[c] = agg[c] + held[recv_pos[c] - cap]
    block = clusters * rc
    lifted = dot3(both[...].reshape(block, -1), up_hi[...], up_lo[...])
    merged = (feat[...].reshape(block, -1) + lifted) * INV_THREE
    v = dot3(merged, dense_hi[...], dense_lo[...])
    result = (merged + v / (1.0 + jnp.exp(-v))) * INV_TWO
    out[...] = result.reshape(out.shape)
    if not last:
        low_out[...] = dot3(result, down[0][...], down[1][...]).reshape(low_out.shape)


def down_kernel(chunks, feat, down, *refs):
    outs, (rows, weight, sems) = refs[:-3], refs[-3:]
    copies = [pltpu.make_async_copy(down.at[0], weight, sems.at[0])]
    for r, (off, rc) in enumerate(chunks):
        part = slice(off, off + rc)
        copies.append(pltpu.make_async_copy(feat.at[:, part, :], rows.at[:, part, :], sems.at[1 + r]))
    for copy in copies:
        copy.start()
    copies[0].wait()
    high, low = split(weight[...])
    for r, (off, rc) in enumerate(chunks):
        copies[1 + r].wait()
        part = rows[:, off : off + rc, :].reshape(-1, rows.shape[-1])
        result = dot3(part, high, low).reshape(-1, rc, weight.shape[-1])
        outs[r][...] = result


def local(
    edge_feat,
    edge_counts,
    reverse,
    patterns,
    trip_count,
    coef,
    down_weight,
    up_weight,
    dense_weight,
):
    clusters, share, feat_width = edge_feat.shape
    layers, _, width = down_weight.shape
    edges, trips, subs = (lax.axis_size(a) for a in ("edge", "trip", "sub"))
    e, x, s = (lax.axis_index(a) for a in ("edge", "trip", "sub"))
    rows = trips * subs * share
    cap = 2 * ((clusters // 2 + edges // 2 - 1) // (edges // 2))
    half_share = share // 2
    chunks = [(0, half_share), (half_share, half_share)]
    n = len(chunks)
    depth = clusters * rows
    slots = patterns.shape[2]
    swap = [(0, 1), (1, 0)]

    def turn(d):
        return [(i, (i + d) % trips) for i in range(trips)]

    ids = jnp.stack([x, s]).astype(jnp.int32)
    coef = coef.reshape(coef.shape[2:])
    coef2 = lax.ppermute(coef, "sub", swap)

    def small(rc):
        return jax.ShapeDtypeStruct((clusters, rc, width), F32)

    def big(rc):
        return jax.ShapeDtypeStruct((clusters, rc, feat_width), F32)

    lows = call(
        functools.partial(down_kernel, chunks),
        [small(rc) for _, rc in chunks],
        [HBM, HBM],
        60,
        flops=6 * clusters * share * feat_width * width,
        scratch=[
            pltpu.VMEM((clusters, share, feat_width), F32),
            pltpu.VMEM((feat_width, width), F32),
            pltpu.SemaphoreType.DMA((1 + n,)),
        ],
    )(edge_feat, down_weight)
    (down_weight, up_weight, dense_weight, reverse, patterns, trip_count, *lows) = lax.optimization_barrier(
        (down_weight, up_weight, dense_weight, reverse, patterns, trip_count, *lows)
    )

    note = jnp.concatenate([patterns.reshape(-1), trip_count.reshape(-1)])
    note = jnp.stack([note, lax.ppermute(note, "sub", swap)])
    here = jnp.arange(clusters, dtype=jnp.int32)
    mine = lax.dynamic_slice_in_dim(reverse, e * clusters, clusters)
    to = mine // clusters
    earlier = (to[:, None] == to[None, :]) & (here[None, :] < here[:, None])
    send_pos = (to ^ e) * cap + jnp.sum(earlier.astype(jnp.int32), axis=1)
    places = jnp.arange(edges * cap, dtype=jnp.int32)
    send_src = jnp.sum(jnp.where(places[:, None] == send_pos[None, :], here[None, :], 0), axis=1)
    everyone = jnp.arange(reverse.shape[0], dtype=jnp.int32)
    before = (
        (everyone[None, :] // clusters == to[:, None])
        & (everyone[None, :] < mine[:, None])
        & ((reverse // clusters)[None, :] == e)
    )
    recv_pos = (to ^ e) * cap + jnp.sum(before.astype(jnp.int32), axis=1)

    def parts(w):
        high = lax.reduce_precision(w, 8, 7)
        return high.astype(BF16), (w - high).astype(BF16)

    down = [parts(down_weight[i]) for i in range(1, layers)]
    up = [parts(up_weight[i]) for i in range(layers)]
    dense = [parts(dense_weight[i]) for i in range(layers)]

    lead_rows = chunks[0][1]
    marks = jnp.pad(note[0].astype(F32), (0, lead_rows * rows - note.shape[1])).reshape(1, lead_rows, rows)

    cells = call(
        functools.partial(cells_kernel, (trips, subs, share, chunks, clusters)),
        [jax.ShapeDtypeStruct((2 * clusters * rc, depth), BF16) for _, rc in chunks]
        + [jax.ShapeDtypeStruct((2 * (trips - 1) * clusters * rc, depth), BF16) for _, rc in chunks]
        + [jax.ShapeDtypeStruct((slots + 1, lead_rows, rows), F32)] * (2 * (trips - 1)),
        [SMEM] * 4 + [HBM] * 3,
        40,
        scratch=[
            pltpu.VMEM((2, trips, slots, share, rows), F32),
            pltpu.VMEM((clusters, trips, clusters, share, rows), F32),
            pltpu.SemaphoreType.DMA((2, trips)),
            pltpu.SemaphoreType.DMA((2 * (trips - 1), 2)),
        ],
        moved=12 << 20,
    )(ids, edge_counts, note[:, :-1], note[:, -1], marks, coef, coef2)
    near, remote, parts = cells[:n], cells[n : 2 * n], cells[2 * n :]

    feats, first = None, None
    for layer in range(layers):
        last = layer == layers - 1
        whole = layer > 0
        order = [0, 1] if whole else [1, 0]
        one, two = first if whole else remote[order[0]], remote[order[1]]
        sizes = [cell.shape[0] // 2 for cell in (one, two)]
        home_depth = subs * clusters * share

        far = [[lax.ppermute(low, "trip", turn(d)) for low in lows] for d in range(1, trips)]
        home = lows + [lax.ppermute(low, "sub", swap) for low in lows]
        home_hi, home_lo, *sides = call(
            functools.partial(home_kernel, n),
            [jax.ShapeDtypeStruct((home_depth, width), BF16)] * 2
            + [jax.ShapeDtypeStruct((size, width), F32) for size in sizes],
            [SMEM] + [VMEM] * (2 + len(home)),
            32,
            flops=6 * sum(sizes) * home_depth * width,
        )(ids, one, two, *home)
        for got in far:
            for r in range(n):
                if layer == 0:
                    got[r], sides[0] = lax.optimization_barrier((got[r], sides[0]))
        far = sum((got + [lax.ppermute(low, "sub", swap) for low in got] for got in far), [])
        if whole:
            outs = [small(chunks[0][1])] + [jax.ShapeDtypeStruct((cap, chunks[0][1], width), F32)] * (edges - 1)
        else:
            outs = [jax.ShapeDtypeStruct((sizes[0], width), F32)]
        far_hi, far_lo, second, *outs = call(
            functools.partial(far_kernel, n, len(far), cap, whole),
            [jax.ShapeDtypeStruct((depth - home_depth, width), BF16)] * 2
            + [jax.ShapeDtypeStruct((sizes[1], width), F32)]
            + outs,
            [SMEM] * 2 + [VMEM] * (4 + len(far)),
            32,
            flops=6 * sum(sizes) * (depth - home_depth) * width,
        )(ids, send_src, one, two, *sides, *far)

        aggs, packs, sums = {}, {}, {}
        if whole:
            aggs[0], *packs[0] = outs
        else:
            sums[order[0]] = outs[0]
        sums[order[1]] = second
        for r, sent in sums.items():
            sent = sent.reshape(trips - 1, clusters, chunks[r][1], width)
            sums[r] = [lax.ppermute(sent[d - 1], "trip", turn(d)) for d in range(1, trips)]
        for r, got in sums.items():
            rc = chunks[r][1]
            own = call(
                near_kernel,
                jax.ShapeDtypeStruct((clusters * rc, width), F32),
                [VMEM] * 5,
                32,
                flops=6 * clusters * rc * depth * width,
            )(home_hi, home_lo, far_hi, far_lo, near[r]).reshape(clusters, rc, width)
            aggs[r], *packs[r] = call(
                functools.partial(pack_kernel, cap, trips - 1),
                [small(rc)] + [jax.ShapeDtypeStruct((cap, rc, width), F32)] * (edges - 1),
                [SMEM] + [VMEM] * trips,
                16,
                moved=4 << 20,
            )(send_src, own, *got)
        if layer == 0:
            off, rc = chunks[0]
            parts, packs[order[-1]] = lax.optimization_barrier((parts, packs[order[-1]]))
            far = []
            for d in range(1, trips):
                for other in range(2):
                    perm = [
                        (i * subs + j, (i + d) % trips * subs + (j ^ other)) for i in range(trips) for j in range(subs)
                    ]
                    far.append(lax.ppermute(parts[2 * (d - 1) + other], ("trip", "sub"), perm))
            notes = jnp.stack([part[slots].reshape(-1)[: note.shape[1]].astype(jnp.int32) for part in far])
            notes = jnp.concatenate([note, notes])
            first = call(
                functools.partial(early_kernel, (trips, subs, share, off, rc, clusters)),
                jax.ShapeDtypeStruct((2 * clusters * rc, depth), BF16),
                [SMEM] * 4 + [HBM] * 2 + [VMEM] * len(far),
                40,
                scratch=[
                    pltpu.VMEM((2, slots, rc, rows), F32),
                    pltpu.VMEM((clusters, 1, clusters, rc, rows), F32),
                    pltpu.SemaphoreType.DMA((2,)),
                ],
                moved=6 << 20,
            )(ids, edge_counts, notes[:, :-1], notes[:, -1], coef, coef2, *far)
        next_feats, next_lows = [None] * n, [None] * n
        result = None
        steps = list(range(edges - 1, 0, -1))
        for i, r in enumerate(order):
            off, rc = chunks[r]
            back = [lax.ppermute(packs[r][k - 1], "edge", [(i, i ^ k) for i in range(edges)]) for k in steps]
            if layer == 0:
                feat, feat_spec = edge_feat, rows_of(clusters, off, rc, feat_width)
            else:
                feat, feat_spec = feats[r], VMEM
            ahead = [packs[later][0] for later in order[i + 1 :]]
            if layer == 0 and i == n - 1:
                ahead.append(first)
            alias = {}
            if last and result is not None:
                alias = {1 + len(ahead): 0}
                ahead.append(result)
            extra = [] if last else down[layer]
            result = call(
                functools.partial(rows_kernel, (clusters, rc, cap, steps), last, len(ahead)),
                big(share) if last else [big(rc), small(rc)],
                [SMEM] + [ANY] * len(ahead) + [feat_spec] + [VMEM] * (1 + edges - 1 + 4 + len(extra)),
                32,
                grid=(1,),
                out_specs=rows_of(clusters, off, rc, feat_width) if last else [VMEM, VMEM],
                scratch=[
                    pltpu.VMEM(((edges - 1) * cap, rc, width), F32),
                    pltpu.VMEM((clusters, rc, width), F32),
                ],
                flops=6 * clusters * rc * feat_width * (2 * width + feat_width),
                alias=alias,
            )(recv_pos, *ahead, feat, aggs[r], *back, *up[layer], *dense[layer], *extra)
            if not last:
                next_feats[r], next_lows[r] = result
        feats, lows = next_feats, next_lows
    return result


def solution(mesh):
    placed = (
        P(("groups", "edge"), ("trip", "sub"), None),
        P(("groups", "edge")),
        P("groups"),
        P(("groups", "edge"), ("trip", "sub"), None, None),
        P(("groups", "edge"), ("trip", "sub")),
        P(("groups", "edge"), ("trip", "sub"), None, None, None),
        P(),
        P(),
        P(),
    )
    return jax.shard_map(
        local,
        mesh=mesh,
        in_specs=placed,
        out_specs=P(("groups", "edge"), ("trip", "sub"), None),
        check_vma=False,
    )
```

```python
import functools

import jax
import jax.numpy as jnp
from jax import lax
from jax.experimental import pallas as pl
from jax.experimental.pallas import tpu as pltpu
from jax.sharding import PartitionSpec as P

INV_THREE = 1.0 / 3.0**0.5
INV_TWO = 1.0 / 2.0**0.5
F32 = jnp.float32
BF16 = jnp.bfloat16
SMEM = pl.BlockSpec(memory_space=pltpu.SMEM)
VMEM = pl.BlockSpec(memory_space=pltpu.VMEM)
ANY = pl.BlockSpec(memory_space=pl.ANY)
HBM = pl.BlockSpec(memory_space=pltpu.HBM)


def split(v):
    high = v.astype(BF16)
    return high, (v - high.astype(F32)).astype(BF16)


def dot(a, b):
    return jnp.dot(a, b, preferred_element_type=F32)


def dot3(a, high, low):
    rows = a.shape[0]
    a_high, a_low = split(a)
    both = dot(jnp.concatenate([a_high, a_low], axis=0), high)
    return both[:rows] + (both[rows:] + dot(a_high, low))


def call(kernel, outs, ins, mib, out_specs=None, scratch=(), flops=0, moved=0, alias=None, grid=()):
    return pl.pallas_call(
        kernel,
        grid=grid,
        out_shape=outs,
        in_specs=ins,
        out_specs=jax.tree.map(lambda _: VMEM, outs) if out_specs is None else out_specs,
        scratch_shapes=list(scratch),
        input_output_aliases=alias or {},
        compiler_params=pltpu.CompilerParams(vmem_limit_bytes=mib << 20),
        cost_estimate=pl.CostEstimate(flops=flops, bytes_accessed=moved, transcendentals=0),
    )


def rows_of(clusters, start, size, width):
    return pl.BlockSpec((clusters, size, width), lambda i: (0, start // size, 0))


def add_cells(acc, pats, live, half, count, slots, load):
    many = 4 if slots % 4 == 0 else 1
    alive = jnp.minimum(live[half], slots)

    def add(i, c):
        found = []
        for p in [many * i + u for u in range(many)]:
            values = [jnp.where(p < alive, load(p, d), 0.0) for d in range(count)]
            found.append((pats[half, 2 * p], pats[half, 2 * p + 1], values))
        for t, q, values in found:
            for d, value in enumerate(values):
                acc[q, d, t] += value
        return c

    lax.fori_loop(0, lax.div(alive + (many - 1), many), add, 0)


def clear(acc):
    zero = jnp.zeros(acc.shape[1:], F32)

    def one(q, c):
        acc[q] = zero
        return c

    lax.fori_loop(0, acc.shape[0], one, 0)


def finish_cells(sizes, x, acc, counts, groups):
    trips, subs, share, clusters = sizes
    width, chip = trips * subs * share, subs * share
    step = clusters // 2

    def finish(g, c):
        for d, off, rc, ref, at in groups:
            block = step * rc
            lane = lax.broadcasted_iota(jnp.int32, (block, width), 1)
            for t in range(0, clusters, step):
                cells = []
                for j in range(trips):
                    cell = acc[g * trips + j, d, t : t + step, off : off + rc, :].reshape(block, width)
                    cells.append(jnp.where(lane < counts[g * trips + j], cell, 0.0))
                bit = 1
                while bit < trips:
                    low_half = lane // chip % (2 * bit) < bit
                    for i in range(trips):
                        if not i & bit:
                            a, b = cells[i], cells[i | bit]
                            cells[i] = jnp.where(low_half, a, pltpu.roll(b, bit * chip, 1))
                            cells[i | bit] = jnp.where(low_half, pltpu.roll(a, width - bit * chip, 1), b)
                    bit *= 2
                for i, cell in enumerate(cells):
                    place = lax.rem(x + trips - i, trips) * clusters * chip + g * width
                    lanes = pl.ds(pl.multiple_of(place, width), width)
                    row = at + t * rc
                    high, low = split(cell)
                    ref[row : row + block, lanes] = high
                    row += ref.shape[0] // 2
                    ref[row : row + block, lanes] = low
        return c

    lax.fori_loop(0, clusters // trips, finish, 0)


def cells_kernel(sizes, ids, counts, pats, live, marks, mine, theirs, *refs):
    trips, subs, share, chunks, clusters = sizes
    n = len(chunks)
    near, remote, parts, (buf, acc, sems, part_sems) = refs[:n], refs[n : 2 * n], refs[2 * n : -4], refs[-4:]
    x, s = ids[0], ids[1]
    slots = mine.shape[0]
    copies, part_copies = [], []
    for half, ref in enumerate((mine, theirs)):
        for d in range(trips):
            start = pl.multiple_of((lax.rem(x + d, trips) * subs + s) * share, share)
            copies.append(
                pltpu.make_async_copy(ref.at[:, pl.ds(start, share), :], buf.at[half, d], sems.at[half, d])
            )
            copies[-1].start()
    off, rc = chunks[0]
    for i, part in enumerate(parts):
        core = 1 - s if i % 2 else s
        start = pl.multiple_of((lax.rem(x + 1 + i // 2, trips) * subs + core) * share + off, rc)
        for k, (src, at, size) in enumerate(((mine.at[:, pl.ds(start, rc), :], 0, slots), (marks, slots, 1))):
            part_copies.append(pltpu.make_async_copy(src, part.at[at : at + size], part_sems.at[i, k]))
            part_copies[-1].start()
    clear(acc)
    for half in range(2):
        for d in range(trips):
            copies[half * trips + d].wait()
        add_cells(acc, pats, live, half, trips, slots, lambda p, d, half=half: buf[half, d, p])
    groups = []
    for r, (off, rc) in enumerate(chunks):
        groups.append((0, off, rc, near[r], 0))
        groups += [(d, off, rc, remote[r], (d - 1) * clusters * rc) for d in range(1, trips)]
    finish_cells((trips, subs, share, clusters), x, acc, counts, groups)
    for copy in part_copies:
        copy.wait()


def early_kernel(sizes, ids, counts, pats, live, mine, theirs, *refs):
    trips, subs, share, off, rc, clusters = sizes
    far, (out, buf, acc, sems) = refs[:-4], refs[-4:]
    slots = mine.shape[0]
    start = pl.multiple_of((ids[0] * subs + ids[1]) * share + off, rc)
    copies = []
    for half, ref in enumerate((mine, theirs)):
        copies.append(pltpu.make_async_copy(ref.at[:, pl.ds(start, rc), :], buf.at[half], sems.at[half]))
        copies[-1].start()
    clear(acc)
    for i, ref in enumerate(far):
        add_cells(acc, pats, live, 2 + i, 1, slots, lambda p, d, ref=ref: ref[p])
    for half in range(2):
        copies[half].wait()
        add_cells(acc, pats, live, half, 1, slots, lambda p, d, half=half: buf[half, p])
    finish_cells((trips, subs, share, clusters), ids[0], acc, counts, [(0, 0, rc, out, 0)])


def terms(cells, x_hi, x_lo, first=0):
    rows = cells.shape[0] // 2
    columns = slice(first, first + x_hi.shape[0])
    both = dot(cells[:, columns], x_hi[...])
    return both[:rows] + (both[rows:] + dot(cells[:rows, columns], x_lo[...]))


def spread(s, n, pieces, x_hi, x_lo):
    clusters = pieces[0].shape[0]
    share = sum(ref.shape[1] for ref in pieces[:n])
    for i in range(0, len(pieces) // n):
        core = 1 - s if i % 2 else s
        for q in range(clusters):
            high, low = split(jnp.concatenate([ref[q] for ref in pieces[i * n : (i + 1) * n]], axis=0))
            at = (i // 2 * clusters + q) * 2 * share + core * share
            spot = pl.ds(pl.multiple_of(at, share), share)
            x_hi[spot, :] = high
            x_lo[spot, :] = low


def near_kernel(home_hi, home_lo, far_hi, far_lo, cells, out):
    out[...] = terms(cells, home_hi, home_lo) + terms(cells, far_hi, far_lo, home_hi.shape[0])


def home_kernel(n, ids, one, two, *refs):
    pieces, (x_hi, x_lo, one_out, two_out) = refs[:-4], refs[-4:]
    spread(ids[1], n, pieces, x_hi, x_lo)
    one_out[...] = terms(one, x_hi, x_lo)
    two_out[...] = terms(two, x_hi, x_lo)


def pack(agg, send_src, cap, packs):
    for k, ref in enumerate(packs):
        for j in range(cap):
            ref[j] = agg[send_src[(k + 1) * cap + j]]


def far_kernel(n, count, cap, whole, ids, send_src, one, two, one_in, two_in, *refs):
    pieces, (x_hi, x_lo, two_out, *outs) = refs[:count], refs[count:]
    first = one.shape[1] - x_hi.shape[0]
    spread(ids[1], n, pieces, x_hi, x_lo)
    out = one_in[...] + terms(one, x_hi, x_lo, first)
    two_out[...] = two_in[...] + terms(two, x_hi, x_lo, first)
    if whole:
        agg, *packs = outs
        agg[...] = out.reshape(agg.shape)
        pack(agg, send_src, cap, packs)
    else:
        outs[0][...] = out


def pack_kernel(cap, arrivals, send_src, local, *refs):
    got, (agg, *packs) = refs[:arrivals], refs[arrivals:]
    total = local[...]
    for ref in got:
        total = total + ref[...]
    agg[...] = total
    pack(agg, send_src, cap, packs)


def rows_kernel(sizes, last, unread, recv_pos, *refs):
    clusters, rc, cap, steps = sizes
    refs = refs[unread:]
    feat, agg, refs = refs[0], refs[1], refs[2:]
    got, refs = refs[: len(steps)], refs[len(steps) :]
    up_hi, up_lo, dense_hi, dense_lo, refs = *refs[:4], refs[4:]
    if last:
        out, held, both = refs
    else:
        down, (out, low_out, held, both) = refs[:2], refs[2:]
    for k, ref in zip(steps, got):
        held[(k - 1) * cap : k * cap] = ref[...]
    for c in range(clusters):
        both[c] = agg[c] + held[recv_pos[c] - cap]
    block = clusters * rc
    lifted = dot3(both[...].reshape(block, -1), up_hi[...], up_lo[...])
    merged = (feat[...].reshape(block, -1) + lifted) * INV_THREE
    v = dot3(merged, dense_hi[...], dense_lo[...])
    result = (merged + v / (1.0 + jnp.exp(-v))) * INV_TWO
    out[...] = result.reshape(out.shape)
    if not last:
        low_out[...] = dot3(result, down[0][...], down[1][...]).reshape(low_out.shape)


def down_kernel(chunks, feat, down, *refs):
    outs, (rows, weight, sems) = refs[:-3], refs[-3:]
    copies = [pltpu.make_async_copy(down.at[0], weight, sems.at[0])]
    for r, (off, rc) in enumerate(chunks):
        part = slice(off, off + rc)
        copies.append(pltpu.make_async_copy(feat.at[:, part, :], rows.at[:, part, :], sems.at[1 + r]))
    for copy in copies:
        copy.start()
    copies[0].wait()
    high, low = split(weight[...])
    for r, (off, rc) in enumerate(chunks):
        copies[1 + r].wait()
        part = rows[:, off : off + rc, :].reshape(-1, rows.shape[-1])
        result = dot3(part, high, low).reshape(-1, rc, weight.shape[-1])
        outs[r][...] = result


def local(
    edge_feat,
    edge_counts,
    reverse,
    patterns,
    trip_count,
    coef,
    down_weight,
    up_weight,
    dense_weight,
):
    clusters, share, feat_width = edge_feat.shape
    layers, _, width = down_weight.shape
    edges, trips, subs = (lax.axis_size(a) for a in ("edge", "trip", "sub"))
    e, x, s = (lax.axis_index(a) for a in ("edge", "trip", "sub"))
    rows = trips * subs * share
    cap = 2 * ((clusters // 2 + edges // 2 - 1) // (edges // 2))
    half_share = share // 2
    chunks = [(0, half_share), (half_share, half_share)]
    n = len(chunks)
    depth = clusters * rows
    slots = patterns.shape[2]
    swap = [(0, 1), (1, 0)]

    def turn(d):
        return [(i, (i + d) % trips) for i in range(trips)]

    ids = jnp.stack([x, s]).astype(jnp.int32)
    coef = coef.reshape(coef.shape[2:])
    coef2 = lax.ppermute(coef, "sub", swap)

    def small(rc):
        return jax.ShapeDtypeStruct((clusters, rc, width), F32)

    def big(rc):
        return jax.ShapeDtypeStruct((clusters, rc, feat_width), F32)

    lows = call(
        functools.partial(down_kernel, chunks),
        [small(rc) for _, rc in chunks],
        [HBM, HBM],
        60,
        flops=6 * clusters * share * feat_width * width,
        scratch=[
            pltpu.VMEM((clusters, share, feat_width), F32),
            pltpu.VMEM((feat_width, width), F32),
            pltpu.SemaphoreType.DMA((1 + n,)),
        ],
    )(edge_feat, down_weight)
    (down_weight, up_weight, dense_weight, reverse, patterns, trip_count, *lows) = lax.optimization_barrier(
        (down_weight, up_weight, dense_weight, reverse, patterns, trip_count, *lows)
    )

    note = jnp.concatenate([patterns.reshape(-1), trip_count.reshape(-1)])
    note = jnp.stack([note, lax.ppermute(note, "sub", swap)])
    here = jnp.arange(clusters, dtype=jnp.int32)
    mine = lax.dynamic_slice_in_dim(reverse, e * clusters, clusters)
    to = mine // clusters
    earlier = (to[:, None] == to[None, :]) & (here[None, :] < here[:, None])
    send_pos = (to ^ e) * cap + jnp.sum(earlier.astype(jnp.int32), axis=1)
    places = jnp.arange(edges * cap, dtype=jnp.int32)
    send_src = jnp.sum(jnp.where(places[:, None] == send_pos[None, :], here[None, :], 0), axis=1)
    everyone = jnp.arange(reverse.shape[0], dtype=jnp.int32)
    before = (
        (everyone[None, :] // clusters == to[:, None])
        & (everyone[None, :] < mine[:, None])
        & ((reverse // clusters)[None, :] == e)
    )
    recv_pos = (to ^ e) * cap + jnp.sum(before.astype(jnp.int32), axis=1)

    def parts(w):
        high = lax.reduce_precision(w, 8, 7)
        return high.astype(BF16), (w - high).astype(BF16)

    down = [parts(down_weight[i]) for i in range(1, layers)]
    up = [parts(up_weight[i]) for i in range(layers)]
    dense = [parts(dense_weight[i]) for i in range(layers)]

    lead_rows = chunks[0][1]
    marks = jnp.pad(note[0].astype(F32), (0, lead_rows * rows - note.shape[1])).reshape(1, lead_rows, rows)

    cells = call(
        functools.partial(cells_kernel, (trips, subs, share, chunks, clusters)),
        [jax.ShapeDtypeStruct((2 * clusters * rc, depth), BF16) for _, rc in chunks]
        + [jax.ShapeDtypeStruct((2 * (trips - 1) * clusters * rc, depth), BF16) for _, rc in chunks]
        + [jax.ShapeDtypeStruct((slots + 1, lead_rows, rows), F32)] * (2 * (trips - 1)),
        [SMEM] * 4 + [HBM] * 3,
        40,
        scratch=[
            pltpu.VMEM((2, trips, slots, share, rows), F32),
            pltpu.VMEM((clusters, trips, clusters, share, rows), F32),
            pltpu.SemaphoreType.DMA((2, trips)),
            pltpu.SemaphoreType.DMA((2 * (trips - 1), 2)),
        ],
        moved=12 << 20,
    )(ids, edge_counts, note[:, :-1], note[:, -1], marks, coef, coef2)
    near, remote, parts = cells[:n], cells[n : 2 * n], cells[2 * n :]

    feats, first = None, None
    for layer in range(layers):
        last = layer == layers - 1
        whole = layer > 0
        order = [0, 1] if whole else [1, 0]
        one, two = first if whole else remote[order[0]], remote[order[1]]
        sizes = [cell.shape[0] // 2 for cell in (one, two)]
        home_depth = subs * clusters * share

        far = [[lax.ppermute(low, "trip", turn(d)) for low in lows] for d in range(1, trips)]
        home = lows + [lax.ppermute(low, "sub", swap) for low in lows]
        home_hi, home_lo, *sides = call(
            functools.partial(home_kernel, n),
            [jax.ShapeDtypeStruct((home_depth, width), BF16)] * 2
            + [jax.ShapeDtypeStruct((size, width), F32) for size in sizes],
            [SMEM] + [VMEM] * (2 + len(home)),
            32,
            flops=6 * sum(sizes) * home_depth * width,
        )(ids, one, two, *home)
        for got in far:
            for r in range(n):
                if layer == 0:
                    got[r], sides[0] = lax.optimization_barrier((got[r], sides[0]))
                elif layer == 1 and r == n - 1:
                    got[r], first = lax.optimization_barrier((got[r], first))
        far = sum((got + [lax.ppermute(low, "sub", swap) for low in got] for got in far), [])
        if whole:
            outs = [small(chunks[0][1])] + [jax.ShapeDtypeStruct((cap, chunks[0][1], width), F32)] * (edges - 1)
        else:
            outs = [jax.ShapeDtypeStruct((sizes[0], width), F32)]
        far_hi, far_lo, second, *outs = call(
            functools.partial(far_kernel, n, len(far), cap, whole),
            [jax.ShapeDtypeStruct((depth - home_depth, width), BF16)] * 2
            + [jax.ShapeDtypeStruct((sizes[1], width), F32)]
            + outs,
            [SMEM] * 2 + [VMEM] * (4 + len(far)),
            32,
            flops=6 * sum(sizes) * (depth - home_depth) * width,
        )(ids, send_src, one, two, *sides, *far)

        aggs, packs, sums = {}, {}, {}
        if whole:
            aggs[0], *packs[0] = outs
        else:
            sums[order[0]] = outs[0]
        sums[order[1]] = second
        for r, sent in sums.items():
            sent = sent.reshape(trips - 1, clusters, chunks[r][1], width)
            sums[r] = [lax.ppermute(sent[d - 1], "trip", turn(d)) for d in range(1, trips)]
        for r, got in sums.items():
            rc = chunks[r][1]
            own = call(
                near_kernel,
                jax.ShapeDtypeStruct((clusters * rc, width), F32),
                [VMEM] * 5,
                32,
                flops=6 * clusters * rc * depth * width,
            )(home_hi, home_lo, far_hi, far_lo, near[r]).reshape(clusters, rc, width)
            aggs[r], *packs[r] = call(
                functools.partial(pack_kernel, cap, trips - 1),
                [small(rc)] + [jax.ShapeDtypeStruct((cap, rc, width), F32)] * (edges - 1),
                [SMEM] + [VMEM] * trips,
                16,
                moved=4 << 20,
            )(send_src, own, *got)
        if layer == 0:
            off, rc = chunks[0]
            parts, packs[order[-1]] = lax.optimization_barrier((parts, packs[order[-1]]))
            far = []
            for d in range(1, trips):
                for other in range(2):
                    perm = [
                        (i * subs + j, (i + d) % trips * subs + (j ^ other)) for i in range(trips) for j in range(subs)
                    ]
                    far.append(lax.ppermute(parts[2 * (d - 1) + other], ("trip", "sub"), perm))
            notes = jnp.stack([part[slots].reshape(-1)[: note.shape[1]].astype(jnp.int32) for part in far])
            notes = jnp.concatenate([note, notes])
            first = call(
                functools.partial(early_kernel, (trips, subs, share, off, rc, clusters)),
                jax.ShapeDtypeStruct((2 * clusters * rc, depth), BF16),
                [SMEM] * 4 + [HBM] * 2 + [VMEM] * len(far),
                40,
                scratch=[
                    pltpu.VMEM((2, slots, rc, rows), F32),
                    pltpu.VMEM((clusters, 1, clusters, rc, rows), F32),
                    pltpu.SemaphoreType.DMA((2,)),
                ],
                moved=6 << 20,
            )(ids, edge_counts, notes[:, :-1], notes[:, -1], coef, coef2, *far)
            fetched = far
        next_feats, next_lows = [None] * n, [None] * n
        result = None
        steps = list(range(edges - 1, 0, -1))
        for i, r in enumerate(order):
            off, rc = chunks[r]
            back = [lax.ppermute(packs[r][k - 1], "edge", [(i, i ^ k) for i in range(edges)]) for k in steps]
            if layer == 0:
                feat, feat_spec = edge_feat, rows_of(clusters, off, rc, feat_width)
            else:
                feat, feat_spec = feats[r], VMEM
            ahead = [packs[later][0] for later in order[i + 1 :]]
            if layer == 0 and i == n - 1:
                ahead.append(notes)
            alias = {}
            if last and result is not None:
                alias = {1 + len(ahead): 0}
                ahead.append(result)
            extra = [] if last else down[layer]
            result = call(
                functools.partial(rows_kernel, (clusters, rc, cap, steps), last, len(ahead)),
                big(share) if last else [big(rc), small(rc)],
                [SMEM] + [ANY] * len(ahead) + [feat_spec] + [VMEM] * (1 + edges - 1 + 4 + len(extra)),
                32,
                grid=(1,),
                out_specs=rows_of(clusters, off, rc, feat_width) if last else [VMEM, VMEM],
                scratch=[
                    pltpu.VMEM(((edges - 1) * cap, rc, width), F32),
                    pltpu.VMEM((clusters, rc, width), F32),
                ],
                flops=6 * clusters * rc * feat_width * (2 * width + feat_width),
                alias=alias,
            )(recv_pos, *ahead, feat, aggs[r], *back, *up[layer], *dense[layer], *extra)
            if not last:
                next_feats[r], next_lows[r] = result
        feats, lows = next_feats, next_lows
    return result


def solution(mesh):
    placed = (
        P(("groups", "edge"), ("trip", "sub"), None),
        P(("groups", "edge")),
        P("groups"),
        P(("groups", "edge"), ("trip", "sub"), None, None),
        P(("groups", "edge"), ("trip", "sub")),
        P(("groups", "edge"), ("trip", "sub"), None, None, None),
        P(),
        P(),
        P(),
    )
    return jax.shard_map(
        local,
        mesh=mesh,
        in_specs=placed,
        out_specs=P(("groups", "edge"), ("trip", "sub"), None),
        check_vma=False,
    )
```

```python
import functools

import jax
import jax.numpy as jnp
from jax import lax
from jax.experimental import pallas as pl
from jax.experimental.pallas import tpu as pltpu
from jax.sharding import PartitionSpec as P

INV_THREE = 1.0 / 3.0**0.5
INV_TWO = 1.0 / 2.0**0.5
F32 = jnp.float32
BF16 = jnp.bfloat16
SMEM = pl.BlockSpec(memory_space=pltpu.SMEM)
VMEM = pl.BlockSpec(memory_space=pltpu.VMEM)
ANY = pl.BlockSpec(memory_space=pl.ANY)
HBM = pl.BlockSpec(memory_space=pltpu.HBM)


def split(v):
    high = v.astype(BF16)
    return high, (v - high.astype(F32)).astype(BF16)


def dot(a, b):
    return jnp.dot(a, b, preferred_element_type=F32)


def dot3(a, high, low):
    rows = a.shape[0]
    a_high, a_low = split(a)
    both = dot(jnp.concatenate([a_high, a_low], axis=0), high)
    return both[:rows] + (both[rows:] + dot(a_high, low))


def call(kernel, outs, ins, mib, out_specs=None, scratch=(), flops=0, moved=0, alias=None, grid=()):
    return pl.pallas_call(
        kernel,
        grid=grid,
        out_shape=outs,
        in_specs=ins,
        out_specs=jax.tree.map(lambda _: VMEM, outs) if out_specs is None else out_specs,
        scratch_shapes=list(scratch),
        input_output_aliases=alias or {},
        compiler_params=pltpu.CompilerParams(vmem_limit_bytes=mib << 20),
        cost_estimate=pl.CostEstimate(flops=flops, bytes_accessed=moved, transcendentals=0),
    )


def rows_of(clusters, start, size, width):
    return pl.BlockSpec((clusters, size, width), lambda i: (0, start // size, 0))


def add_cells(acc, pats, live, half, count, slots, load):
    many = 4 if slots % 4 == 0 else 1
    alive = jnp.minimum(live[half], slots)

    def add(i, c):
        found = []
        for p in [many * i + u for u in range(many)]:
            values = [jnp.where(p < alive, load(p, d), 0.0) for d in range(count)]
            found.append((pats[half, 2 * p], pats[half, 2 * p + 1], values))
        for t, q, values in found:
            for d, value in enumerate(values):
                acc[q, d, t] += value
        return c

    lax.fori_loop(0, lax.div(alive + (many - 1), many), add, 0)


def clear(acc):
    zero = jnp.zeros(acc.shape[1:], F32)

    def one(q, c):
        acc[q] = zero
        return c

    lax.fori_loop(0, acc.shape[0], one, 0)


def finish_cells(sizes, x, acc, counts, groups):
    trips, subs, share, clusters = sizes
    width, chip = trips * subs * share, subs * share
    step = clusters // 2

    def finish(g, c):
        for d, off, rc, ref, at in groups:
            block = step * rc
            lane = lax.broadcasted_iota(jnp.int32, (block, width), 1)
            for t in range(0, clusters, step):
                cells = []
                for j in range(trips):
                    cell = acc[g * trips + j, d, t : t + step, off : off + rc, :].reshape(block, width)
                    cells.append(jnp.where(lane < counts[g * trips + j], cell, 0.0))
                bit = 1
                while bit < trips:
                    low_half = lane // chip % (2 * bit) < bit
                    for i in range(trips):
                        if not i & bit:
                            a, b = cells[i], cells[i | bit]
                            cells[i] = jnp.where(low_half, a, pltpu.roll(b, bit * chip, 1))
                            cells[i | bit] = jnp.where(low_half, pltpu.roll(a, width - bit * chip, 1), b)
                    bit *= 2
                for i, cell in enumerate(cells):
                    place = lax.rem(x + trips - i, trips) * clusters * chip + g * width
                    lanes = pl.ds(pl.multiple_of(place, width), width)
                    row = at + t * rc
                    high, low = split(cell)
                    ref[row : row + block, lanes] = high
                    row += ref.shape[0] // 2
                    ref[row : row + block, lanes] = low
        return c

    lax.fori_loop(0, clusters // trips, finish, 0)


def cells_kernel(sizes, ids, counts, pats, live, marks, mine, theirs, *refs):
    trips, subs, share, chunks, clusters = sizes
    n = len(chunks)
    near, remote, parts, (buf, acc, sems, part_sems) = refs[:n], refs[n : 2 * n], refs[2 * n : -4], refs[-4:]
    x, s = ids[0], ids[1]
    slots = mine.shape[0]
    copies, part_copies = [], []
    for half, ref in enumerate((mine, theirs)):
        for d in range(trips):
            start = pl.multiple_of((lax.rem(x + d, trips) * subs + s) * share, share)
            copies.append(
                pltpu.make_async_copy(ref.at[:, pl.ds(start, share), :], buf.at[half, d], sems.at[half, d])
            )
            copies[-1].start()
    off, rc = chunks[0]
    for i, part in enumerate(parts):
        core = 1 - s if i % 2 else s
        start = pl.multiple_of((lax.rem(x + 1 + i // 2, trips) * subs + core) * share + off, rc)
        for k, (src, at, size) in enumerate(((mine.at[:, pl.ds(start, rc), :], 0, slots), (marks, slots, 1))):
            part_copies.append(pltpu.make_async_copy(src, part.at[at : at + size], part_sems.at[i, k]))
            part_copies[-1].start()
    clear(acc)
    for half in range(2):
        for d in range(trips):
            copies[half * trips + d].wait()
        add_cells(acc, pats, live, half, trips, slots, lambda p, d, half=half: buf[half, d, p])
    groups = []
    for r, (off, rc) in enumerate(chunks):
        groups.append((0, off, rc, near[r], 0))
        groups += [(d, off, rc, remote[r], (d - 1) * clusters * rc) for d in range(1, trips)]
    finish_cells((trips, subs, share, clusters), x, acc, counts, groups)
    for copy in part_copies:
        copy.wait()


def early_kernel(sizes, ids, counts, pats, live, mine, theirs, *refs):
    trips, subs, share, off, rc, clusters = sizes
    far, (out, buf, acc, sems) = refs[:-4], refs[-4:]
    slots = mine.shape[0]
    start = pl.multiple_of((ids[0] * subs + ids[1]) * share + off, rc)
    copies = []
    for half, ref in enumerate((mine, theirs)):
        copies.append(pltpu.make_async_copy(ref.at[:, pl.ds(start, rc), :], buf.at[half], sems.at[half]))
        copies[-1].start()
    clear(acc)
    for i, ref in enumerate(far):
        add_cells(acc, pats, live, 2 + i, 1, slots, lambda p, d, ref=ref: ref[p])
    for half in range(2):
        copies[half].wait()
        add_cells(acc, pats, live, half, 1, slots, lambda p, d, half=half: buf[half, p])
    finish_cells((trips, subs, share, clusters), ids[0], acc, counts, [(0, 0, rc, out, 0)])


def terms(cells, x_hi, x_lo, first=0):
    rows = cells.shape[0] // 2
    columns = slice(first, first + x_hi.shape[0])
    both = dot(cells[:, columns], x_hi[...])
    return both[:rows] + (both[rows:] + dot(cells[:rows, columns], x_lo[...]))


def spread(s, n, pieces, x_hi, x_lo):
    clusters = pieces[0].shape[0]
    share = sum(ref.shape[1] for ref in pieces[:n])
    for i in range(0, len(pieces) // n):
        core = 1 - s if i % 2 else s
        for q in range(clusters):
            high, low = split(jnp.concatenate([ref[q] for ref in pieces[i * n : (i + 1) * n]], axis=0))
            at = (i // 2 * clusters + q) * 2 * share + core * share
            spot = pl.ds(pl.multiple_of(at, share), share)
            x_hi[spot, :] = high
            x_lo[spot, :] = low


def near_kernel(home_hi, home_lo, far_hi, far_lo, cells, out):
    out[...] = terms(cells, home_hi, home_lo) + terms(cells, far_hi, far_lo, home_hi.shape[0])


def home_kernel(n, ids, one, two, *refs):
    pieces, (x_hi, x_lo, one_out, two_out) = refs[:-4], refs[-4:]
    spread(ids[1], n, pieces, x_hi, x_lo)
    one_out[...] = terms(one, x_hi, x_lo)
    two_out[...] = terms(two, x_hi, x_lo)


def pack(agg, send_src, cap, packs):
    for k, ref in enumerate(packs):
        for j in range(cap):
            ref[j] = agg[send_src[(k + 1) * cap + j]]


def far_kernel(n, count, cap, whole, ids, send_src, one, two, one_in, two_in, *refs):
    pieces, (x_hi, x_lo, two_out, *outs) = refs[:count], refs[count:]
    first = one.shape[1] - x_hi.shape[0]
    spread(ids[1], n, pieces, x_hi, x_lo)
    out = one_in[...] + terms(one, x_hi, x_lo, first)
    two_out[...] = two_in[...] + terms(two, x_hi, x_lo, first)
    if whole:
        agg, *packs = outs
        agg[...] = out.reshape(agg.shape)
        pack(agg, send_src, cap, packs)
    else:
        outs[0][...] = out


def pack_kernel(cap, arrivals, send_src, local, *refs):
    got, (agg, *packs) = refs[:arrivals], refs[arrivals:]
    total = local[...]
    for ref in got:
        total = total + ref[...]
    agg[...] = total
    pack(agg, send_src, cap, packs)


def rows_kernel(sizes, last, unread, recv_pos, *refs):
    clusters, rc, cap, steps = sizes
    refs = refs[unread:]
    feat, agg, refs = refs[0], refs[1], refs[2:]
    got, refs = refs[: len(steps)], refs[len(steps) :]
    up_hi, up_lo, dense_hi, dense_lo, refs = *refs[:4], refs[4:]
    if last:
        out, held, both = refs
    else:
        down, (out, low_out, held, both) = refs[:2], refs[2:]
    for k, ref in zip(steps, got):
        held[(k - 1) * cap : k * cap] = ref[...]
    for c in range(clusters):
        both[c] = agg[c] + held[recv_pos[c] - cap]
    block = clusters * rc
    lifted = dot3(both[...].reshape(block, -1), up_hi[...], up_lo[...])
    merged = (feat[...].reshape(block, -1) + lifted) * INV_THREE
    v = dot3(merged, dense_hi[...], dense_lo[...])
    result = (merged + v / (1.0 + jnp.exp(-v))) * INV_TWO
    out[...] = result.reshape(out.shape)
    if not last:
        low_out[...] = dot3(result, down[0][...], down[1][...]).reshape(low_out.shape)


def down_kernel(chunks, feat, down, *refs):
    outs, (rows, weight, sems) = refs[:-3], refs[-3:]
    copies = [pltpu.make_async_copy(down.at[0], weight, sems.at[0])]
    for r, (off, rc) in enumerate(chunks):
        part = slice(off, off + rc)
        copies.append(pltpu.make_async_copy(feat.at[:, part, :], rows.at[:, part, :], sems.at[1 + r]))
    for copy in copies:
        copy.start()
    copies[0].wait()
    high, low = split(weight[...])
    for r, (off, rc) in enumerate(chunks):
        copies[1 + r].wait()
        part = rows[:, off : off + rc, :].reshape(-1, rows.shape[-1])
        result = dot3(part, high, low).reshape(-1, rc, weight.shape[-1])
        outs[r][...] = result


def local(
    edge_feat,
    edge_counts,
    reverse,
    patterns,
    trip_count,
    coef,
    down_weight,
    up_weight,
    dense_weight,
):
    clusters, share, feat_width = edge_feat.shape
    layers, _, width = down_weight.shape
    edges, trips, subs = (lax.axis_size(a) for a in ("edge", "trip", "sub"))
    e, x, s = (lax.axis_index(a) for a in ("edge", "trip", "sub"))
    rows = trips * subs * share
    cap = 2 * ((clusters // 2 + edges // 2 - 1) // (edges // 2))
    half_share = share // 2
    chunks = [(0, half_share), (half_share, half_share)]
    n = len(chunks)
    depth = clusters * rows
    slots = patterns.shape[2]
    swap = [(0, 1), (1, 0)]

    def turn(d):
        return [(i, (i + d) % trips) for i in range(trips)]

    ids = jnp.stack([x, s]).astype(jnp.int32)
    coef = coef.reshape(coef.shape[2:])
    coef2 = lax.ppermute(coef, "sub", swap)

    def small(rc):
        return jax.ShapeDtypeStruct((clusters, rc, width), F32)

    def big(rc):
        return jax.ShapeDtypeStruct((clusters, rc, feat_width), F32)

    lows = call(
        functools.partial(down_kernel, chunks),
        [small(rc) for _, rc in chunks],
        [HBM, HBM],
        60,
        flops=6 * clusters * share * feat_width * width,
        scratch=[
            pltpu.VMEM((clusters, share, feat_width), F32),
            pltpu.VMEM((feat_width, width), F32),
            pltpu.SemaphoreType.DMA((1 + n,)),
        ],
    )(edge_feat, down_weight)
    (down_weight, up_weight, dense_weight, reverse, patterns, trip_count, *lows) = lax.optimization_barrier(
        (down_weight, up_weight, dense_weight, reverse, patterns, trip_count, *lows)
    )

    note = jnp.concatenate([patterns.reshape(-1), trip_count.reshape(-1)])
    note = jnp.stack([note, lax.ppermute(note, "sub", swap)])
    here = jnp.arange(clusters, dtype=jnp.int32)
    mine = lax.dynamic_slice_in_dim(reverse, e * clusters, clusters)
    to = mine // clusters
    earlier = (to[:, None] == to[None, :]) & (here[None, :] < here[:, None])
    send_pos = (to ^ e) * cap + jnp.sum(earlier.astype(jnp.int32), axis=1)
    places = jnp.arange(edges * cap, dtype=jnp.int32)
    send_src = jnp.sum(jnp.where(places[:, None] == send_pos[None, :], here[None, :], 0), axis=1)
    everyone = jnp.arange(reverse.shape[0], dtype=jnp.int32)
    before = (
        (everyone[None, :] // clusters == to[:, None])
        & (everyone[None, :] < mine[:, None])
        & ((reverse // clusters)[None, :] == e)
    )
    recv_pos = (to ^ e) * cap + jnp.sum(before.astype(jnp.int32), axis=1)

    def parts(w):
        high = lax.reduce_precision(w, 8, 7)
        return high.astype(BF16), (w - high).astype(BF16)

    down = [parts(down_weight[i]) for i in range(1, layers)]
    up = [parts(up_weight[i]) for i in range(layers)]
    dense = [parts(dense_weight[i]) for i in range(layers)]

    lead_rows = chunks[0][1]
    marks = jnp.pad(note[0].astype(F32), (0, lead_rows * rows - note.shape[1])).reshape(1, lead_rows, rows)

    cells = call(
        functools.partial(cells_kernel, (trips, subs, share, chunks, clusters)),
        [jax.ShapeDtypeStruct((2 * clusters * rc, depth), BF16) for _, rc in chunks]
        + [jax.ShapeDtypeStruct((2 * (trips - 1) * clusters * rc, depth), BF16) for _, rc in chunks]
        + [jax.ShapeDtypeStruct((slots + 1, lead_rows, rows), F32)] * (2 * (trips - 1)),
        [SMEM] * 4 + [HBM] * 3,
        40,
        scratch=[
            pltpu.VMEM((2, trips, slots, share, rows), F32),
            pltpu.VMEM((clusters, trips, clusters, share, rows), F32),
            pltpu.SemaphoreType.DMA((2, trips)),
            pltpu.SemaphoreType.DMA((2 * (trips - 1), 2)),
        ],
        moved=12 << 20,
    )(ids, edge_counts, note[:, :-1], note[:, -1], marks, coef, coef2)
    near, remote, parts = list(cells[:n]), cells[n : 2 * n], cells[2 * n :]

    feats, first = None, None
    for layer in range(layers):
        last = layer == layers - 1
        whole = layer > 0
        order = [0, 1] if whole else [1, 0]
        one, two = first if whole else remote[order[0]], remote[order[1]]
        sizes = [cell.shape[0] // 2 for cell in (one, two)]
        home_depth = subs * clusters * share

        far = [[lax.ppermute(low, "trip", turn(d)) for low in lows] for d in range(1, trips)]
        home = lows + [lax.ppermute(low, "sub", swap) for low in lows]
        home_hi, home_lo, *sides = call(
            functools.partial(home_kernel, n),
            [jax.ShapeDtypeStruct((home_depth, width), BF16)] * 2
            + [jax.ShapeDtypeStruct((size, width), F32) for size in sizes],
            [SMEM] + [VMEM] * (2 + len(home)),
            32,
            flops=6 * sum(sizes) * home_depth * width,
        )(ids, one, two, *home)
        for got in far:
            for r in range(n):
                if layer == 0:
                    got[r], near[0] = lax.optimization_barrier((got[r], near[0]))
                elif layer == 1 and r == n - 1:
                    got[r], first = lax.optimization_barrier((got[r], first))
        far = sum((got + [lax.ppermute(low, "sub", swap) for low in got] for got in far), [])
        if whole:
            outs = [small(chunks[0][1])] + [jax.ShapeDtypeStruct((cap, chunks[0][1], width), F32)] * (edges - 1)
        else:
            outs = [jax.ShapeDtypeStruct((sizes[0], width), F32)]
        far_hi, far_lo, second, *outs = call(
            functools.partial(far_kernel, n, len(far), cap, whole),
            [jax.ShapeDtypeStruct((depth - home_depth, width), BF16)] * 2
            + [jax.ShapeDtypeStruct((sizes[1], width), F32)]
            + outs,
            [SMEM] * 2 + [VMEM] * (4 + len(far)),
            32,
            flops=6 * sum(sizes) * (depth - home_depth) * width,
        )(ids, send_src, one, two, *sides, *far)

        aggs, packs, sums = {}, {}, {}
        if whole:
            aggs[0], *packs[0] = outs
        else:
            sums[order[0]] = outs[0]
        sums[order[1]] = second
        for r, sent in sums.items():
            sent = sent.reshape(trips - 1, clusters, chunks[r][1], width)
            sums[r] = [lax.ppermute(sent[d - 1], "trip", turn(d)) for d in range(1, trips)]
        for r, got in sums.items():
            rc = chunks[r][1]
            own = call(
                near_kernel,
                jax.ShapeDtypeStruct((clusters * rc, width), F32),
                [VMEM] * 5,
                32,
                flops=6 * clusters * rc * depth * width,
            )(home_hi, home_lo, far_hi, far_lo, near[r]).reshape(clusters, rc, width)
            aggs[r], *packs[r] = call(
                functools.partial(pack_kernel, cap, trips - 1),
                [small(rc)] + [jax.ShapeDtypeStruct((cap, rc, width), F32)] * (edges - 1),
                [SMEM] + [VMEM] * trips,
                16,
                moved=4 << 20,
            )(send_src, own, *got)
        if layer == 0:
            off, rc = chunks[0]
            parts, packs[order[-1]] = lax.optimization_barrier((parts, packs[order[-1]]))
            far = []
            for d in range(1, trips):
                for other in range(2):
                    perm = [
                        (i * subs + j, (i + d) % trips * subs + (j ^ other)) for i in range(trips) for j in range(subs)
                    ]
                    far.append(lax.ppermute(parts[2 * (d - 1) + other], ("trip", "sub"), perm))
            notes = jnp.stack([part[slots].reshape(-1)[: note.shape[1]].astype(jnp.int32) for part in far])
            notes = jnp.concatenate([note, notes])
            first = call(
                functools.partial(early_kernel, (trips, subs, share, off, rc, clusters)),
                jax.ShapeDtypeStruct((2 * clusters * rc, depth), BF16),
                [SMEM] * 4 + [HBM] * 2 + [VMEM] * len(far),
                40,
                scratch=[
                    pltpu.VMEM((2, slots, rc, rows), F32),
                    pltpu.VMEM((clusters, 1, clusters, rc, rows), F32),
                    pltpu.SemaphoreType.DMA((2,)),
                ],
                moved=6 << 20,
            )(ids, edge_counts, notes[:, :-1], notes[:, -1], coef, coef2, *far)
            fetched = far
        next_feats, next_lows = [None] * n, [None] * n
        result = None
        steps = sorted(range(1, edges), key=lambda k: (layer == 0 or k != edges // 2, -k))
        for i, r in enumerate(order):
            off, rc = chunks[r]
            back = [lax.ppermute(packs[r][k - 1], "edge", [(i, i ^ k) for i in range(edges)]) for k in steps]
            if layer == 0:
                feat, feat_spec = edge_feat, rows_of(clusters, off, rc, feat_width)
            else:
                feat, feat_spec = feats[r], VMEM
            ahead = [packs[later][0] for later in order[i + 1 :]]
            if layer == 0 and i == n - 1:
                ahead.append(notes)
            alias = {}
            if last and result is not None:
                alias = {1 + len(ahead): 0}
                ahead.append(result)
            extra = [] if last else down[layer]
            result = call(
                functools.partial(rows_kernel, (clusters, rc, cap, steps), last, len(ahead)),
                big(share) if last else [big(rc), small(rc)],
                [SMEM] + [ANY] * len(ahead) + [feat_spec] + [VMEM] * (1 + edges - 1 + 4 + len(extra)),
                32,
                grid=(1,),
                out_specs=rows_of(clusters, off, rc, feat_width) if last else [VMEM, VMEM],
                scratch=[
                    pltpu.VMEM(((edges - 1) * cap, rc, width), F32),
                    pltpu.VMEM((clusters, rc, width), F32),
                ],
                flops=6 * clusters * rc * feat_width * (2 * width + feat_width),
                alias=alias,
            )(recv_pos, *ahead, feat, aggs[r], *back, *up[layer], *dense[layer], *extra)
            if not last:
                next_feats[r], next_lows[r] = result
        feats, lows = next_feats, next_lows
    return result


def solution(mesh):
    placed = (
        P(("groups", "edge"), ("trip", "sub"), None),
        P(("groups", "edge")),
        P("groups"),
        P(("groups", "edge"), ("trip", "sub"), None, None),
        P(("groups", "edge"), ("trip", "sub")),
        P(("groups", "edge"), ("trip", "sub"), None, None, None),
        P(),
        P(),
        P(),
    )
    return jax.shard_map(
        local,
        mesh=mesh,
        in_specs=placed,
        out_specs=P(("groups", "edge"), ("trip", "sub"), None),
        check_vma=False,
    )
```

```python
import functools

import jax
import jax.numpy as jnp
from jax import lax
from jax.experimental import pallas as pl
from jax.experimental.pallas import tpu as pltpu
from jax.sharding import PartitionSpec as P

INV_THREE = 1.0 / 3.0**0.5
INV_TWO = 1.0 / 2.0**0.5
F32 = jnp.float32
BF16 = jnp.bfloat16
SMEM = pl.BlockSpec(memory_space=pltpu.SMEM)
VMEM = pl.BlockSpec(memory_space=pltpu.VMEM)
ANY = pl.BlockSpec(memory_space=pl.ANY)
HBM = pl.BlockSpec(memory_space=pltpu.HBM)


def split(v):
    high = v.astype(BF16)
    return high, (v - high.astype(F32)).astype(BF16)


def dot(a, b):
    return jnp.dot(a, b, preferred_element_type=F32)


def dot3(a, high, low):
    rows = a.shape[0]
    a_high, a_low = split(a)
    both = dot(jnp.concatenate([a_high, a_low], axis=0), high)
    return both[:rows] + (both[rows:] + dot(a_high, low))


def call(kernel, outs, ins, mib, out_specs=None, scratch=(), flops=0, moved=0, alias=None, grid=()):
    return pl.pallas_call(
        kernel,
        grid=grid,
        out_shape=outs,
        in_specs=ins,
        out_specs=jax.tree.map(lambda _: VMEM, outs) if out_specs is None else out_specs,
        scratch_shapes=list(scratch),
        input_output_aliases=alias or {},
        compiler_params=pltpu.CompilerParams(vmem_limit_bytes=mib << 20),
        cost_estimate=pl.CostEstimate(flops=flops, bytes_accessed=moved, transcendentals=0),
    )


def rows_of(clusters, start, size, width):
    return pl.BlockSpec((clusters, size, width), lambda i: (0, start // size, 0))


def add_cells(acc, pats, live, half, count, slots, load):
    many = 4 if slots % 4 == 0 else 1
    alive = jnp.minimum(live[half], slots)

    def add(i, c):
        found = []
        for p in [many * i + u for u in range(many)]:
            values = [jnp.where(p < alive, load(p, d), 0.0) for d in range(count)]
            found.append((pats[half, 2 * p], pats[half, 2 * p + 1], values))
        for t, q, values in found:
            for d, value in enumerate(values):
                acc[q, d, t] += value
        return c

    lax.fori_loop(0, lax.div(alive + (many - 1), many), add, 0)


def clear(acc):
    zero = jnp.zeros(acc.shape[1:], F32)

    def one(q, c):
        acc[q] = zero
        return c

    lax.fori_loop(0, acc.shape[0], one, 0)


def finish_cells(sizes, x, acc, counts, groups):
    trips, subs, share, clusters = sizes
    width, chip = trips * subs * share, subs * share
    step = clusters // 2

    def finish(g, c):
        for d, off, rc, ref, at in groups:
            block = step * rc
            lane = lax.broadcasted_iota(jnp.int32, (block, width), 1)
            for t in range(0, clusters, step):
                cells = []
                for j in range(trips):
                    cell = acc[g * trips + j, d, t : t + step, off : off + rc, :].reshape(block, width)
                    cells.append(jnp.where(lane < counts[g * trips + j], cell, 0.0))
                bit = 1
                while bit < trips:
                    low_half = lane // chip % (2 * bit) < bit
                    for i in range(trips):
                        if not i & bit:
                            a, b = cells[i], cells[i | bit]
                            cells[i] = jnp.where(low_half, a, pltpu.roll(b, bit * chip, 1))
                            cells[i | bit] = jnp.where(low_half, pltpu.roll(a, width - bit * chip, 1), b)
                    bit *= 2
                for i, cell in enumerate(cells):
                    place = lax.rem(x + trips - i, trips) * clusters * chip + g * width
                    lanes = pl.ds(pl.multiple_of(place, width), width)
                    row = at + t * rc
                    high, low = split(cell)
                    ref[row : row + block, lanes] = high
                    row += ref.shape[0] // 2
                    ref[row : row + block, lanes] = low
        return c

    lax.fori_loop(0, clusters // trips, finish, 0)


def cells_kernel(sizes, ids, counts, pats, live, marks, mine, theirs, *refs):
    trips, subs, share, chunks, clusters = sizes
    n = len(chunks)
    near, remote, parts, (buf, acc, sems, part_sems) = refs[:n], refs[n : 2 * n], refs[2 * n : -4], refs[-4:]
    x, s = ids[0], ids[1]
    slots = mine.shape[0]
    copies, part_copies = [], []
    for half, ref in enumerate((mine, theirs)):
        for d in range(trips):
            start = pl.multiple_of((lax.rem(x + d, trips) * subs + s) * share, share)
            copies.append(
                pltpu.make_async_copy(ref.at[:, pl.ds(start, share), :], buf.at[half, d], sems.at[half, d])
            )
            copies[-1].start()
    off, rc = chunks[0]
    for i, part in enumerate(parts):
        core = 1 - s if i % 2 else s
        start = pl.multiple_of((lax.rem(x + 1 + i // 2, trips) * subs + core) * share + off, rc)
        for k, (src, at, size) in enumerate(((mine.at[:, pl.ds(start, rc), :], 0, slots), (marks, slots, 1))):
            part_copies.append(pltpu.make_async_copy(src, part.at[at : at + size], part_sems.at[i, k]))
            part_copies[-1].start()
    clear(acc)
    for half in range(2):
        for d in range(trips):
            copies[half * trips + d].wait()
        add_cells(acc, pats, live, half, trips, slots, lambda p, d, half=half: buf[half, d, p])
    groups = []
    for r, (off, rc) in enumerate(chunks):
        groups.append((0, off, rc, near[r], 0))
        groups += [(d, off, rc, remote[r], (d - 1) * clusters * rc) for d in range(1, trips)]
    finish_cells((trips, subs, share, clusters), x, acc, counts, groups)
    for copy in part_copies:
        copy.wait()


def early_kernel(sizes, ids, counts, pats, live, mine, theirs, *refs):
    trips, subs, share, off, rc, clusters = sizes
    far, (out, buf, acc, sems) = refs[:-4], refs[-4:]
    slots = mine.shape[0]
    start = pl.multiple_of((ids[0] * subs + ids[1]) * share + off, rc)
    copies = []
    for half, ref in enumerate((mine, theirs)):
        copies.append(pltpu.make_async_copy(ref.at[:, pl.ds(start, rc), :], buf.at[half], sems.at[half]))
        copies[-1].start()
    clear(acc)
    for i, ref in enumerate(far):
        add_cells(acc, pats, live, 2 + i, 1, slots, lambda p, d, ref=ref: ref[p])
    for half in range(2):
        copies[half].wait()
        add_cells(acc, pats, live, half, 1, slots, lambda p, d, half=half: buf[half, p])
    finish_cells((trips, subs, share, clusters), ids[0], acc, counts, [(0, 0, rc, out, 0)])


def terms(cells, x_hi, x_lo, first=0):
    rows = cells.shape[0] // 2
    columns = slice(first, first + x_hi.shape[0])
    both = dot(cells[:, columns], x_hi[...])
    return both[:rows] + (both[rows:] + dot(cells[:rows, columns], x_lo[...]))


def spread(s, n, pieces, x_hi, x_lo):
    clusters = pieces[0].shape[0]
    share = sum(ref.shape[1] for ref in pieces[:n])
    for i in range(0, len(pieces) // n):
        core = 1 - s if i % 2 else s
        for q in range(clusters):
            high, low = split(jnp.concatenate([ref[q] for ref in pieces[i * n : (i + 1) * n]], axis=0))
            at = (i // 2 * clusters + q) * 2 * share + core * share
            spot = pl.ds(pl.multiple_of(at, share), share)
            x_hi[spot, :] = high
            x_lo[spot, :] = low


def near_kernel(home_hi, home_lo, far_hi, far_lo, cells, out):
    out[...] = terms(cells, home_hi, home_lo) + terms(cells, far_hi, far_lo, home_hi.shape[0])


def home_kernel(n, ids, one, two, *refs):
    pieces, (x_hi, x_lo, one_out, two_out) = refs[:-4], refs[-4:]
    spread(ids[1], n, pieces, x_hi, x_lo)
    one_out[...] = terms(one, x_hi, x_lo)
    two_out[...] = terms(two, x_hi, x_lo)


def pack(agg, send_src, cap, packs):
    for k, ref in enumerate(packs):
        for j in range(cap):
            ref[j] = agg[send_src[(k + 1) * cap + j]]


def far_kernel(n, count, cap, whole, ids, send_src, one, two, one_in, two_in, *refs):
    pieces, (x_hi, x_lo, two_out, *outs) = refs[:count], refs[count:]
    first = one.shape[1] - x_hi.shape[0]
    spread(ids[1], n, pieces, x_hi, x_lo)
    out = one_in[...] + terms(one, x_hi, x_lo, first)
    two_out[...] = two_in[...] + terms(two, x_hi, x_lo, first)
    if whole:
        agg, *packs = outs
        agg[...] = out.reshape(agg.shape)
        pack(agg, send_src, cap, packs)
    else:
        outs[0][...] = out


def pack_kernel(cap, arrivals, send_src, local, *refs):
    got, (agg, *packs) = refs[:arrivals], refs[arrivals:]
    total = local[...]
    for ref in got:
        total = total + ref[...]
    agg[...] = total
    pack(agg, send_src, cap, packs)


def rows_kernel(sizes, last, unread, recv_pos, *refs):
    clusters, rc, cap, steps = sizes
    refs = refs[unread:]
    feat, agg, refs = refs[0], refs[1], refs[2:]
    got, refs = refs[: len(steps)], refs[len(steps) :]
    up_hi, up_lo, dense_hi, dense_lo, refs = *refs[:4], refs[4:]
    if last:
        out, held, both = refs
    else:
        down, (out, low_out, held, both) = refs[:2], refs[2:]
    for k, ref in zip(steps, got):
        held[(k - 1) * cap : k * cap] = ref[...]
    for c in range(clusters):
        both[c] = agg[c] + held[recv_pos[c] - cap]
    block = clusters * rc
    lifted = dot3(both[...].reshape(block, -1), up_hi[...], up_lo[...])
    merged = (feat[...].reshape(block, -1) + lifted) * INV_THREE
    v = dot3(merged, dense_hi[...], dense_lo[...])
    result = (merged + v / (1.0 + jnp.exp(-v))) * INV_TWO
    out[...] = result.reshape(out.shape)
    if not last:
        low_out[...] = dot3(result, down[0][...], down[1][...]).reshape(low_out.shape)


def down_kernel(chunks, feat, down, *refs):
    outs, (rows, weight, sems) = refs[:-3], refs[-3:]
    copies = [pltpu.make_async_copy(down.at[0], weight, sems.at[0])]
    for r, (off, rc) in enumerate(chunks):
        part = slice(off, off + rc)
        copies.append(pltpu.make_async_copy(feat.at[:, part, :], rows.at[:, part, :], sems.at[1 + r]))
    for copy in copies:
        copy.start()
    copies[0].wait()
    high, low = split(weight[...])
    for r, (off, rc) in enumerate(chunks):
        copies[1 + r].wait()
        part = rows[:, off : off + rc, :].reshape(-1, rows.shape[-1])
        result = dot3(part, high, low).reshape(-1, rc, weight.shape[-1])
        outs[r][...] = result


def local(
    edge_feat,
    edge_counts,
    reverse,
    patterns,
    trip_count,
    coef,
    down_weight,
    up_weight,
    dense_weight,
):
    clusters, share, feat_width = edge_feat.shape
    layers, _, width = down_weight.shape
    edges, trips, subs = (lax.axis_size(a) for a in ("edge", "trip", "sub"))
    e, x, s = (lax.axis_index(a) for a in ("edge", "trip", "sub"))
    rows = trips * subs * share
    cap = 2 * ((clusters // 2 + edges // 2 - 1) // (edges // 2))
    half_share = share // 2
    chunks = [(0, half_share), (half_share, half_share)]
    n = len(chunks)
    depth = clusters * rows
    slots = patterns.shape[2]
    swap = [(0, 1), (1, 0)]

    def turn(d):
        return [(i, (i + d) % trips) for i in range(trips)]

    ids = jnp.stack([x, s]).astype(jnp.int32)
    coef = coef.reshape(coef.shape[2:])
    coef2 = lax.ppermute(coef, "sub", swap)

    def small(rc):
        return jax.ShapeDtypeStruct((clusters, rc, width), F32)

    def big(rc):
        return jax.ShapeDtypeStruct((clusters, rc, feat_width), F32)

    lows = call(
        functools.partial(down_kernel, chunks),
        [small(rc) for _, rc in chunks],
        [HBM, HBM],
        60,
        flops=6 * clusters * share * feat_width * width,
        scratch=[
            pltpu.VMEM((clusters, share, feat_width), F32),
            pltpu.VMEM((feat_width, width), F32),
            pltpu.SemaphoreType.DMA((1 + n,)),
        ],
    )(edge_feat, down_weight)
    (down_weight, up_weight, dense_weight, reverse, patterns, trip_count, *lows) = lax.optimization_barrier(
        (down_weight, up_weight, dense_weight, reverse, patterns, trip_count, *lows)
    )

    note = jnp.concatenate([patterns.reshape(-1), trip_count.reshape(-1)])
    note = jnp.stack([note, lax.ppermute(note, "sub", swap)])
    here = jnp.arange(clusters, dtype=jnp.int32)
    mine = lax.dynamic_slice_in_dim(reverse, e * clusters, clusters)
    to = mine // clusters
    earlier = (to[:, None] == to[None, :]) & (here[None, :] < here[:, None])
    send_pos = (to ^ e) * cap + jnp.sum(earlier.astype(jnp.int32), axis=1)
    places = jnp.arange(edges * cap, dtype=jnp.int32)
    send_src = jnp.sum(jnp.where(places[:, None] == send_pos[None, :], here[None, :], 0), axis=1)
    everyone = jnp.arange(reverse.shape[0], dtype=jnp.int32)
    before = (
        (everyone[None, :] // clusters == to[:, None])
        & (everyone[None, :] < mine[:, None])
        & ((reverse // clusters)[None, :] == e)
    )
    recv_pos = (to ^ e) * cap + jnp.sum(before.astype(jnp.int32), axis=1)

    def parts(w):
        high = lax.reduce_precision(w, 8, 7)
        return high.astype(BF16), (w - high).astype(BF16)

    down = [parts(down_weight[i]) for i in range(1, layers)]
    up = [parts(up_weight[i]) for i in range(layers)]
    dense = [parts(dense_weight[i]) for i in range(layers)]

    lead_rows = chunks[0][1]
    marks = jnp.pad(note[0].astype(F32), (0, lead_rows * rows - note.shape[1])).reshape(1, lead_rows, rows)

    cells = call(
        functools.partial(cells_kernel, (trips, subs, share, chunks, clusters)),
        [jax.ShapeDtypeStruct((2 * clusters * rc, depth), BF16) for _, rc in chunks]
        + [jax.ShapeDtypeStruct((2 * (trips - 1) * clusters * rc, depth), BF16) for _, rc in chunks]
        + [jax.ShapeDtypeStruct((slots + 1, lead_rows, rows), F32)] * (2 * (trips - 1)),
        [SMEM] * 4 + [HBM] * 3,
        40,
        scratch=[
            pltpu.VMEM((2, trips, slots, share, rows), F32),
            pltpu.VMEM((clusters, trips, clusters, share, rows), F32),
            pltpu.SemaphoreType.DMA((2, trips)),
            pltpu.SemaphoreType.DMA((2 * (trips - 1), 2)),
        ],
        moved=12 << 20,
    )(ids, edge_counts, note[:, :-1], note[:, -1], marks, coef, coef2)
    near, remote, parts = list(cells[:n]), cells[n : 2 * n], cells[2 * n :]

    feats, first = None, None
    for layer in range(layers):
        last = layer == layers - 1
        whole = layer > 0
        order = [0, 1] if whole else [1, 0]
        one, two = first if whole else remote[order[0]], remote[order[1]]
        sizes = [cell.shape[0] // 2 for cell in (one, two)]
        home_depth = subs * clusters * share

        far = [[lax.ppermute(low, "trip", turn(d)) for low in lows] for d in range(1, trips)]
        home = lows + [lax.ppermute(low, "sub", swap) for low in lows]
        home_hi, home_lo, *sides = call(
            functools.partial(home_kernel, n),
            [jax.ShapeDtypeStruct((home_depth, width), BF16)] * 2
            + [jax.ShapeDtypeStruct((size, width), F32) for size in sizes],
            [SMEM] + [VMEM] * (2 + len(home)),
            32,
            flops=6 * sum(sizes) * home_depth * width,
        )(ids, one, two, *home)
        for got in far:
            for r in range(n):
                if layer == 0:
                    got[r], near[0] = lax.optimization_barrier((got[r], near[0]))
                elif layer == 1 and r == n - 1:
                    got[r], first = lax.optimization_barrier((got[r], first))
        far = sum((got + [lax.ppermute(low, "sub", swap) for low in got] for got in far), [])
        if whole:
            outs = [small(chunks[0][1])] + [jax.ShapeDtypeStruct((cap, chunks[0][1], width), F32)] * (edges - 1)
        else:
            outs = [jax.ShapeDtypeStruct((sizes[0], width), F32)]
        far_hi, far_lo, second, *outs = call(
            functools.partial(far_kernel, n, len(far), cap, whole),
            [jax.ShapeDtypeStruct((depth - home_depth, width), BF16)] * 2
            + [jax.ShapeDtypeStruct((sizes[1], width), F32)]
            + outs,
            [SMEM] * 2 + [VMEM] * (4 + len(far)),
            32,
            flops=6 * sum(sizes) * (depth - home_depth) * width,
        )(ids, send_src, one, two, *sides, *far)

        aggs, packs, sums = {}, {}, {}
        if whole:
            aggs[0], *packs[0] = outs
        else:
            sums[order[0]] = outs[0]
        sums[order[1]] = second
        for r, sent in sums.items():
            sent = sent.reshape(trips - 1, clusters, chunks[r][1], width)
            sums[r] = [lax.ppermute(sent[d - 1], "trip", turn(d)) for d in range(1, trips)]
        for r, got in sums.items():
            rc = chunks[r][1]
            own = call(
                near_kernel,
                jax.ShapeDtypeStruct((clusters * rc, width), F32),
                [VMEM] * 5,
                32,
                flops=6 * clusters * rc * depth * width,
            )(home_hi, home_lo, far_hi, far_lo, near[r]).reshape(clusters, rc, width)
            aggs[r], *packs[r] = call(
                functools.partial(pack_kernel, cap, trips - 1),
                [small(rc)] + [jax.ShapeDtypeStruct((cap, rc, width), F32)] * (edges - 1),
                [SMEM] + [VMEM] * trips,
                16,
                moved=4 << 20,
            )(send_src, own, *got)
        if layer == 0:
            off, rc = chunks[0]
            parts, packs[order[-1]] = lax.optimization_barrier((parts, packs[order[-1]]))
            far = []
            for d in range(1, trips):
                for other in range(2):
                    perm = [
                        (i * subs + j, (i + d) % trips * subs + (j ^ other)) for i in range(trips) for j in range(subs)
                    ]
                    far.append(lax.ppermute(parts[2 * (d - 1) + other], ("trip", "sub"), perm))
            notes = jnp.stack([part[slots].reshape(-1)[: note.shape[1]].astype(jnp.int32) for part in far])
            notes = jnp.concatenate([note, notes])
            first = call(
                functools.partial(early_kernel, (trips, subs, share, off, rc, clusters)),
                jax.ShapeDtypeStruct((2 * clusters * rc, depth), BF16),
                [SMEM] * 4 + [HBM] * 2 + [VMEM] * len(far),
                40,
                scratch=[
                    pltpu.VMEM((2, slots, rc, rows), F32),
                    pltpu.VMEM((clusters, 1, clusters, rc, rows), F32),
                    pltpu.SemaphoreType.DMA((2,)),
                ],
                moved=6 << 20,
            )(ids, edge_counts, notes[:, :-1], notes[:, -1], coef, coef2, *far)
            fetched = far
        next_feats, next_lows = [None] * n, [None] * n
        result = None
        if layer == 0:
            steps = [edges - 1, *range(1, edges - 1)]
        else:
            steps = sorted(range(1, edges), key=lambda k: (k != edges // 2, -k))
        for i, r in enumerate(order):
            off, rc = chunks[r]
            back = [lax.ppermute(packs[r][k - 1], "edge", [(i, i ^ k) for i in range(edges)]) for k in steps]
            if layer == 0:
                feat, feat_spec = edge_feat, rows_of(clusters, off, rc, feat_width)
            else:
                feat, feat_spec = feats[r], VMEM
            ahead = [packs[later][0] for later in order[i + 1 :]]
            if layer == 0 and i == n - 1:
                ahead.append(notes)
            alias = {}
            if last and result is not None:
                alias = {1 + len(ahead): 0}
                ahead.append(result)
            extra = [] if last else down[layer]
            result = call(
                functools.partial(rows_kernel, (clusters, rc, cap, steps), last, len(ahead)),
                big(share) if last else [big(rc), small(rc)],
                [SMEM] + [ANY] * len(ahead) + [feat_spec] + [VMEM] * (1 + edges - 1 + 4 + len(extra)),
                32,
                grid=(1,),
                out_specs=rows_of(clusters, off, rc, feat_width) if last else [VMEM, VMEM],
                scratch=[
                    pltpu.VMEM(((edges - 1) * cap, rc, width), F32),
                    pltpu.VMEM((clusters, rc, width), F32),
                ],
                flops=6 * clusters * rc * feat_width * (2 * width + feat_width),
                alias=alias,
            )(recv_pos, *ahead, feat, aggs[r], *back, *up[layer], *dense[layer], *extra)
            if not last:
                next_feats[r], next_lows[r] = result
        feats, lows = next_feats, next_lows
    return result


def solution(mesh):
    placed = (
        P(("groups", "edge"), ("trip", "sub"), None),
        P(("groups", "edge")),
        P("groups"),
        P(("groups", "edge"), ("trip", "sub"), None, None),
        P(("groups", "edge"), ("trip", "sub")),
        P(("groups", "edge"), ("trip", "sub"), None, None, None),
        P(),
        P(),
        P(),
    )
    return jax.shard_map(
        local,
        mesh=mesh,
        in_specs=placed,
        out_specs=P(("groups", "edge"), ("trip", "sub"), None),
        check_vma=False,
    )
```

```python
import functools

import jax
import jax.numpy as jnp
from jax import lax
from jax.experimental import pallas as pl
from jax.experimental.pallas import tpu as pltpu
from jax.sharding import PartitionSpec as P

INV_THREE = 1.0 / 3.0**0.5
INV_TWO = 1.0 / 2.0**0.5
F32 = jnp.float32
BF16 = jnp.bfloat16
SMEM = pl.BlockSpec(memory_space=pltpu.SMEM)
VMEM = pl.BlockSpec(memory_space=pltpu.VMEM)
ANY = pl.BlockSpec(memory_space=pl.ANY)
HBM = pl.BlockSpec(memory_space=pltpu.HBM)


def split(v):
    high = v.astype(BF16)
    return high, (v - high.astype(F32)).astype(BF16)


def dot(a, b):
    return jnp.dot(a, b, preferred_element_type=F32)


def dot3(a, high, low):
    rows = a.shape[0]
    a_high, a_low = split(a)
    both = dot(jnp.concatenate([a_high, a_low], axis=0), high)
    return both[:rows] + (both[rows:] + dot(a_high, low))


def call(kernel, outs, ins, mib, out_specs=None, scratch=(), flops=0, moved=0, alias=None, grid=()):
    return pl.pallas_call(
        kernel,
        grid=grid,
        out_shape=outs,
        in_specs=ins,
        out_specs=jax.tree.map(lambda _: VMEM, outs) if out_specs is None else out_specs,
        scratch_shapes=list(scratch),
        input_output_aliases=alias or {},
        compiler_params=pltpu.CompilerParams(vmem_limit_bytes=mib << 20),
        cost_estimate=pl.CostEstimate(flops=flops, bytes_accessed=moved, transcendentals=0),
    )


def rows_of(clusters, start, size, width):
    return pl.BlockSpec((clusters, size, width), lambda i: (0, start // size, 0))


def add_cells(acc, pats, live, half, count, slots, load):
    many = 4 if slots % 4 == 0 else 1
    alive = jnp.minimum(live[half], slots)

    def add(i, c):
        found = []
        for p in [many * i + u for u in range(many)]:
            values = [jnp.where(p < alive, load(p, d), 0.0) for d in range(count)]
            found.append((pats[half, 2 * p], pats[half, 2 * p + 1], values))
        for t, q, values in found:
            for d, value in enumerate(values):
                acc[q, d, t] += value
        return c

    lax.fori_loop(0, lax.div(alive + (many - 1), many), add, 0)


def clear(acc):
    zero = jnp.zeros(acc.shape[1:], F32)

    def one(q, c):
        acc[q] = zero
        return c

    lax.fori_loop(0, acc.shape[0], one, 0)


def finish_cells(sizes, x, acc, counts, groups):
    trips, subs, share, clusters = sizes
    width, chip = trips * subs * share, subs * share
    step = clusters // 2

    def finish(g, c):
        for d, off, rc, ref, at in groups:
            block = step * rc
            lane = lax.broadcasted_iota(jnp.int32, (block, width), 1)
            for t in range(0, clusters, step):
                cells = []
                for j in range(trips):
                    cell = acc[g * trips + j, d, t : t + step, off : off + rc, :].reshape(block, width)
                    cells.append(jnp.where(lane < counts[g * trips + j], cell, 0.0))
                bit = 1
                while bit < trips:
                    low_half = lane // chip % (2 * bit) < bit
                    for i in range(trips):
                        if not i & bit:
                            a, b = cells[i], cells[i | bit]
                            cells[i] = jnp.where(low_half, a, pltpu.roll(b, bit * chip, 1))
                            cells[i | bit] = jnp.where(low_half, pltpu.roll(a, width - bit * chip, 1), b)
                    bit *= 2
                for i, cell in enumerate(cells):
                    place = lax.rem(x + trips - i, trips) * clusters * chip + g * width
                    lanes = pl.ds(pl.multiple_of(place, width), width)
                    row = at + t * rc
                    high, low = split(cell)
                    ref[row : row + block, lanes] = high
                    row += ref.shape[0] // 2
                    ref[row : row + block, lanes] = low
        return c

    lax.fori_loop(0, clusters // trips, finish, 0)


def cells_kernel(sizes, ids, counts, pats, live, marks, mine, theirs, *refs):
    trips, subs, share, chunks, clusters = sizes
    n = len(chunks)
    near, remote, parts, (buf, acc, sems, part_sems) = refs[:n], refs[n : 2 * n], refs[2 * n : -4], refs[-4:]
    x, s = ids[0], ids[1]
    slots = mine.shape[0]
    copies, part_copies = [], []
    for half, ref in enumerate((mine, theirs)):
        for d in range(trips):
            start = pl.multiple_of((lax.rem(x + d, trips) * subs + s) * share, share)
            copies.append(
                pltpu.make_async_copy(ref.at[:, pl.ds(start, share), :], buf.at[half, d], sems.at[half, d])
            )
            copies[-1].start()
    off, rc = chunks[0]
    for i, part in enumerate(parts):
        core = 1 - s if i % 2 else s
        start = pl.multiple_of((lax.rem(x + 1 + i // 2, trips) * subs + core) * share + off, rc)
        for k, (src, at, size) in enumerate(((mine.at[:, pl.ds(start, rc), :], 0, slots), (marks, slots, 1))):
            part_copies.append(pltpu.make_async_copy(src, part.at[at : at + size], part_sems.at[i, k]))
            part_copies[-1].start()
    clear(acc)
    for half in range(2):
        for d in range(trips):
            copies[half * trips + d].wait()
        add_cells(acc, pats, live, half, trips, slots, lambda p, d, half=half: buf[half, d, p])
    groups = []
    for r, (off, rc) in enumerate(chunks):
        groups.append((0, off, rc, near[r], 0))
        groups += [(d, off, rc, remote[r], (d - 1) * clusters * rc) for d in range(1, trips)]
    finish_cells((trips, subs, share, clusters), x, acc, counts, groups)
    for copy in part_copies:
        copy.wait()


def early_kernel(sizes, ids, counts, pats, live, mine, theirs, *refs):
    trips, subs, share, off, rc, clusters = sizes
    far, (out, buf, acc, sems) = refs[:-4], refs[-4:]
    slots = mine.shape[0]
    start = pl.multiple_of((ids[0] * subs + ids[1]) * share + off, rc)
    copies = []
    for half, ref in enumerate((mine, theirs)):
        copies.append(pltpu.make_async_copy(ref.at[:, pl.ds(start, rc), :], buf.at[half], sems.at[half]))
        copies[-1].start()
    clear(acc)
    for i, ref in enumerate(far):
        add_cells(acc, pats, live, 2 + i, 1, slots, lambda p, d, ref=ref: ref[p])
    for half in range(2):
        copies[half].wait()
        add_cells(acc, pats, live, half, 1, slots, lambda p, d, half=half: buf[half, p])
    finish_cells((trips, subs, share, clusters), ids[0], acc, counts, [(0, 0, rc, out, 0)])


def terms(cells, x_hi, x_lo, first=0):
    rows = cells.shape[0] // 2
    columns = slice(first, first + x_hi.shape[0])
    both = dot(cells[:, columns], x_hi[...])
    return both[:rows] + (both[rows:] + dot(cells[:rows, columns], x_lo[...]))


def spread(s, n, pieces, x_hi, x_lo):
    clusters = pieces[0].shape[0]
    share = sum(ref.shape[1] for ref in pieces[:n])
    for i in range(0, len(pieces) // n):
        core = 1 - s if i % 2 else s
        for q in range(clusters):
            high, low = split(jnp.concatenate([ref[q] for ref in pieces[i * n : (i + 1) * n]], axis=0))
            at = (i // 2 * clusters + q) * 2 * share + core * share
            spot = pl.ds(pl.multiple_of(at, share), share)
            x_hi[spot, :] = high
            x_lo[spot, :] = low


def near_kernel(home_hi, home_lo, far_hi, far_lo, cells, out):
    out[...] = terms(cells, home_hi, home_lo) + terms(cells, far_hi, far_lo, home_hi.shape[0])


def home_kernel(n, ids, one, two, *refs):
    pieces, (x_hi, x_lo, one_out, two_out) = refs[:-4], refs[-4:]
    spread(ids[1], n, pieces, x_hi, x_lo)
    one_out[...] = terms(one, x_hi, x_lo)
    two_out[...] = terms(two, x_hi, x_lo)


def pack(agg, send_src, cap, packs):
    for k, ref in enumerate(packs):
        for j in range(cap):
            ref[j] = agg[send_src[(k + 1) * cap + j]]


def far_kernel(n, count, cap, whole, ids, send_src, one, two, one_in, two_in, *refs):
    pieces, (x_hi, x_lo, two_out, *outs) = refs[:count], refs[count:]
    first = one.shape[1] - x_hi.shape[0]
    spread(ids[1], n, pieces, x_hi, x_lo)
    out = one_in[...] + terms(one, x_hi, x_lo, first)
    two_out[...] = two_in[...] + terms(two, x_hi, x_lo, first)
    if whole:
        agg, *packs = outs
        agg[...] = out.reshape(agg.shape)
        pack(agg, send_src, cap, packs)
    else:
        outs[0][...] = out


def pack_kernel(cap, arrivals, send_src, local, *refs):
    got, (agg, *packs) = refs[:arrivals], refs[arrivals:]
    total = local[...]
    for ref in got:
        total = total + ref[...]
    agg[...] = total
    pack(agg, send_src, cap, packs)


def rows_kernel(sizes, last, unread, recv_pos, *refs):
    clusters, rc, cap, steps = sizes
    refs = refs[unread:]
    feat, agg, refs = refs[0], refs[1], refs[2:]
    got, refs = refs[: len(steps)], refs[len(steps) :]
    up_hi, up_lo, dense_hi, dense_lo, refs = *refs[:4], refs[4:]
    if last:
        out, held, both = refs
    else:
        down, (out, low_out, held, both) = refs[:2], refs[2:]
    for k, ref in zip(steps, got):
        held[(k - 1) * cap : k * cap] = ref[...]
    for c in range(clusters):
        both[c] = agg[c] + held[recv_pos[c] - cap]
    block = clusters * rc
    lifted = dot3(both[...].reshape(block, -1), up_hi[...], up_lo[...])
    merged = (feat[...].reshape(block, -1) + lifted) * INV_THREE
    v = dot3(merged, dense_hi[...], dense_lo[...])
    result = (merged + v / (1.0 + jnp.exp(-v))) * INV_TWO
    out[...] = result.reshape(out.shape)
    if not last:
        low_out[...] = dot3(result, down[0][...], down[1][...]).reshape(low_out.shape)


def down_kernel(chunks, feat, down, *refs):
    outs, (rows, weight, sems) = refs[:-3], refs[-3:]
    copies = [pltpu.make_async_copy(down.at[0], weight, sems.at[0])]
    for r, (off, rc) in enumerate(chunks):
        part = slice(off, off + rc)
        copies.append(pltpu.make_async_copy(feat.at[:, part, :], rows.at[:, part, :], sems.at[1 + r]))
    for copy in copies:
        copy.start()
    copies[0].wait()
    high, low = split(weight[...])
    for r, (off, rc) in enumerate(chunks):
        copies[1 + r].wait()
        part = rows[:, off : off + rc, :].reshape(-1, rows.shape[-1])
        result = dot3(part, high, low).reshape(-1, rc, weight.shape[-1])
        outs[r][...] = result


def local(
    edge_feat,
    edge_counts,
    reverse,
    patterns,
    trip_count,
    coef,
    down_weight,
    up_weight,
    dense_weight,
):
    clusters, share, feat_width = edge_feat.shape
    layers, _, width = down_weight.shape
    edges, trips, subs = (lax.axis_size(a) for a in ("edge", "trip", "sub"))
    e, x, s = (lax.axis_index(a) for a in ("edge", "trip", "sub"))
    rows = trips * subs * share
    cap = 2 * ((clusters // 2 + edges // 2 - 1) // (edges // 2))
    half_share = share // 2
    chunks = [(0, half_share), (half_share, half_share)]
    n = len(chunks)
    depth = clusters * rows
    slots = patterns.shape[2]
    swap = [(0, 1), (1, 0)]

    def turn(d):
        return [(i, (i + d) % trips) for i in range(trips)]

    ids = jnp.stack([x, s]).astype(jnp.int32)
    coef = coef.reshape(coef.shape[2:])
    coef2 = lax.ppermute(coef, "sub", swap)

    def small(rc):
        return jax.ShapeDtypeStruct((clusters, rc, width), F32)

    def big(rc):
        return jax.ShapeDtypeStruct((clusters, rc, feat_width), F32)

    lows = call(
        functools.partial(down_kernel, chunks),
        [small(rc) for _, rc in chunks],
        [HBM, HBM],
        60,
        flops=6 * clusters * share * feat_width * width,
        scratch=[
            pltpu.VMEM((clusters, share, feat_width), F32),
            pltpu.VMEM((feat_width, width), F32),
            pltpu.SemaphoreType.DMA((1 + n,)),
        ],
    )(edge_feat, down_weight)
    (down_weight, up_weight, dense_weight, reverse, patterns, trip_count, *lows) = lax.optimization_barrier(
        (down_weight, up_weight, dense_weight, reverse, patterns, trip_count, *lows)
    )

    note = jnp.concatenate([patterns.reshape(-1), trip_count.reshape(-1)])
    note = jnp.stack([note, lax.ppermute(note, "sub", swap)])
    here = jnp.arange(clusters, dtype=jnp.int32)
    mine = lax.dynamic_slice_in_dim(reverse, e * clusters, clusters)
    to = mine // clusters
    earlier = (to[:, None] == to[None, :]) & (here[None, :] < here[:, None])
    send_pos = (to ^ e) * cap + jnp.sum(earlier.astype(jnp.int32), axis=1)
    places = jnp.arange(edges * cap, dtype=jnp.int32)
    send_src = jnp.sum(jnp.where(places[:, None] == send_pos[None, :], here[None, :], 0), axis=1)
    everyone = jnp.arange(reverse.shape[0], dtype=jnp.int32)
    before = (
        (everyone[None, :] // clusters == to[:, None])
        & (everyone[None, :] < mine[:, None])
        & ((reverse // clusters)[None, :] == e)
    )
    recv_pos = (to ^ e) * cap + jnp.sum(before.astype(jnp.int32), axis=1)

    def parts(w):
        high = lax.reduce_precision(w, 8, 7)
        return high.astype(BF16), (w - high).astype(BF16)

    down = [parts(down_weight[i]) for i in range(1, layers)]
    up = [parts(up_weight[i]) for i in range(layers)]
    dense = [parts(dense_weight[i]) for i in range(layers)]

    lead_rows = chunks[0][1]
    marks = jnp.pad(note[0].astype(F32), (0, lead_rows * rows - note.shape[1])).reshape(1, lead_rows, rows)

    cells = call(
        functools.partial(cells_kernel, (trips, subs, share, chunks, clusters)),
        [jax.ShapeDtypeStruct((2 * clusters * rc, depth), BF16) for _, rc in chunks]
        + [jax.ShapeDtypeStruct((2 * (trips - 1) * clusters * rc, depth), BF16) for _, rc in chunks]
        + [jax.ShapeDtypeStruct((slots + 1, lead_rows, rows), F32)] * (2 * (trips - 1)),
        [SMEM] * 4 + [HBM] * 3,
        40,
        scratch=[
            pltpu.VMEM((2, trips, slots, share, rows), F32),
            pltpu.VMEM((clusters, trips, clusters, share, rows), F32),
            pltpu.SemaphoreType.DMA((2, trips)),
            pltpu.SemaphoreType.DMA((2 * (trips - 1), 2)),
        ],
        moved=12 << 20,
    )(ids, edge_counts, note[:, :-1], note[:, -1], marks, coef, coef2)
    near, remote, parts = list(cells[:n]), cells[n : 2 * n], cells[2 * n :]

    feats, first = None, None
    for layer in range(layers):
        last = layer == layers - 1
        whole = layer > 0
        order = [0, 1] if whole else [1, 0]
        one, two = first if whole else remote[order[0]], remote[order[1]]
        sizes = [cell.shape[0] // 2 for cell in (one, two)]
        home_depth = subs * clusters * share

        far = [[lax.ppermute(low, "trip", turn(d)) for low in lows] for d in range(1, trips)]
        home = lows + [lax.ppermute(low, "sub", swap) for low in lows]
        home_hi, home_lo, *sides = call(
            functools.partial(home_kernel, n),
            [jax.ShapeDtypeStruct((home_depth, width), BF16)] * 2
            + [jax.ShapeDtypeStruct((size, width), F32) for size in sizes],
            [SMEM] + [VMEM] * (2 + len(home)),
            32,
            flops=6 * sum(sizes) * home_depth * width,
        )(ids, one, two, *home)
        for got in far:
            for r in range(n):
                if layer == 0:
                    got[r], near[0] = lax.optimization_barrier((got[r], near[0]))
                elif layer == 1 and r == n - 1:
                    got[r], first = lax.optimization_barrier((got[r], first))
        far = sum((got + [lax.ppermute(low, "sub", swap) for low in got] for got in far), [])
        if whole:
            outs = [small(chunks[0][1])] + [jax.ShapeDtypeStruct((cap, chunks[0][1], width), F32)] * (edges - 1)
        else:
            outs = [jax.ShapeDtypeStruct((sizes[0], width), F32)]
        far_hi, far_lo, second, *outs = call(
            functools.partial(far_kernel, n, len(far), cap, whole),
            [jax.ShapeDtypeStruct((depth - home_depth, width), BF16)] * 2
            + [jax.ShapeDtypeStruct((sizes[1], width), F32)]
            + outs,
            [SMEM] * 2 + [VMEM] * (4 + len(far)),
            32,
            flops=6 * sum(sizes) * (depth - home_depth) * width,
        )(ids, send_src, one, two, *sides, *far)

        aggs, packs, sums = {}, {}, {}
        if whole:
            aggs[0], *packs[0] = outs
        else:
            sums[order[0]] = outs[0]
        sums[order[1]] = second
        for r, sent in sums.items():
            sent = sent.reshape(trips - 1, clusters, chunks[r][1], width)
            sums[r] = [lax.ppermute(sent[d - 1], "trip", turn(d)) for d in range(1, trips)]
        for r, got in sums.items():
            rc = chunks[r][1]
            own = call(
                near_kernel,
                jax.ShapeDtypeStruct((clusters * rc, width), F32),
                [VMEM] * 5,
                32,
                flops=6 * clusters * rc * depth * width,
            )(home_hi, home_lo, far_hi, far_lo, near[r]).reshape(clusters, rc, width)
            aggs[r], *packs[r] = call(
                functools.partial(pack_kernel, cap, trips - 1),
                [small(rc)] + [jax.ShapeDtypeStruct((cap, rc, width), F32)] * (edges - 1),
                [SMEM] + [VMEM] * trips,
                16,
                moved=4 << 20,
            )(send_src, own, *got)
        if layer == 0:
            off, rc = chunks[0]
            parts, packs[order[-1]] = lax.optimization_barrier((parts, packs[order[-1]]))
            far = []
            for d in range(1, trips):
                for other in range(2):
                    perm = [
                        (i * subs + j, (i + d) % trips * subs + (j ^ other)) for i in range(trips) for j in range(subs)
                    ]
                    far.append(lax.ppermute(parts[2 * (d - 1) + other], ("trip", "sub"), perm))
            notes = jnp.stack([part[slots].reshape(-1)[: note.shape[1]].astype(jnp.int32) for part in far])
            notes = jnp.concatenate([note, notes])
            first = call(
                functools.partial(early_kernel, (trips, subs, share, off, rc, clusters)),
                jax.ShapeDtypeStruct((2 * clusters * rc, depth), BF16),
                [SMEM] * 4 + [HBM] * 2 + [VMEM] * len(far),
                40,
                scratch=[
                    pltpu.VMEM((2, slots, rc, rows), F32),
                    pltpu.VMEM((clusters, 1, clusters, rc, rows), F32),
                    pltpu.SemaphoreType.DMA((2,)),
                ],
                moved=6 << 20,
            )(ids, edge_counts, notes[:, :-1], notes[:, -1], coef, coef2, *far)
            fetched = far
        next_feats, next_lows = [None] * n, [None] * n
        result = None
        if layer == 0:
            steps = [edges - 1, *range(1, edges - 1)]
        else:
            steps = sorted(range(1, edges), key=lambda k: (k != edges // 2, k if last else -k))
        for i, r in enumerate(order):
            off, rc = chunks[r]
            back = [lax.ppermute(packs[r][k - 1], "edge", [(i, i ^ k) for i in range(edges)]) for k in steps]
            if layer == 0:
                feat, feat_spec = edge_feat, rows_of(clusters, off, rc, feat_width)
            else:
                feat, feat_spec = feats[r], VMEM
            ahead = [packs[later][0] for later in order[i + 1 :]]
            if layer == 0 and i == n - 1:
                ahead.append(notes)
            alias = {}
            if last and result is not None:
                alias = {1 + len(ahead): 0}
                ahead.append(result)
            extra = [] if last else down[layer]
            result = call(
                functools.partial(rows_kernel, (clusters, rc, cap, steps), last, len(ahead)),
                big(share) if last else [big(rc), small(rc)],
                [SMEM] + [ANY] * len(ahead) + [feat_spec] + [VMEM] * (1 + edges - 1 + 4 + len(extra)),
                32,
                grid=(1,),
                out_specs=rows_of(clusters, off, rc, feat_width) if last else [VMEM, VMEM],
                scratch=[
                    pltpu.VMEM(((edges - 1) * cap, rc, width), F32),
                    pltpu.VMEM((clusters, rc, width), F32),
                ],
                flops=6 * clusters * rc * feat_width * (2 * width + feat_width),
                alias=alias,
            )(recv_pos, *ahead, feat, aggs[r], *back, *up[layer], *dense[layer], *extra)
            if not last:
                next_feats[r], next_lows[r] = result
        feats, lows = next_feats, next_lows
    return result


def solution(mesh):
    placed = (
        P(("groups", "edge"), ("trip", "sub"), None),
        P(("groups", "edge")),
        P("groups"),
        P(("groups", "edge"), ("trip", "sub"), None, None),
        P(("groups", "edge"), ("trip", "sub")),
        P(("groups", "edge"), ("trip", "sub"), None, None, None),
        P(),
        P(),
        P(),
    )
    return jax.shard_map(
        local,
        mesh=mesh,
        in_specs=placed,
        out_specs=P(("groups", "edge"), ("trip", "sub"), None),
        check_vma=False,
    )
```
